32 devices in a mesh: fsdp: 8 (over z, y), rep: 4 (over x, core).
Axes of the slice: x: 2, y: 2, z: 4, core: 2. Of those that a mesh axis runs over, the one named last changes fastest.
Arguments:
- anchors: float32 [3, 1024], P(None, ('fsdp', 'rep')), may hold values from -4 to 4
- directions: float32 [3, 1024], P(None, ('fsdp', 'rep')), may hold values from -4 to 4
- deltas: float32 [1024, 128], P(('fsdp', 'rep')), may hold values from 0.02 to 0.1
- foreground: int32 [1024, 128], P(('fsdp', 'rep')), may hold values from 0 to 1, as said below
- sdf_first_dir: bfloat16 [39, 256], P(None, ('fsdp', 'rep')), may hold values from -1 to 1
- sdf_first_gain: bfloat16 [256], P(('fsdp', 'rep')), may hold values from 0.5 to 2
- sdf_first_bias: bfloat16 [256], P(('fsdp', 'rep')), may hold values from -1.5 to 1.5
- sdf_mid_dir: bfloat16 [4, 256, 256], P(None, None, ('fsdp', 'rep')), may hold values from -0.375 to 0.375
- sdf_mid_gain: bfloat16 [4, 256], P(None, ('fsdp', 'rep')), may hold values from 0.5 to 2
- sdf_mid_bias: bfloat16 [4, 256], P(None, ('fsdp', 'rep')), may hold values from -1.5 to 1.5
- sdf_narrow_dir: bfloat16 [256, 217], P(('fsdp', 'rep')), may hold values from -0.375 to 0.375
- sdf_narrow_gain: bfloat16 [217], replicated, may hold values from 0.5 to 2
- sdf_narrow_bias: bfloat16 [217], replicated, may hold values from -1.5 to 1.5
- sdf_skip_dir: bfloat16 [256, 256], P(None, ('fsdp', 'rep')), may hold values from -0.375 to 0.375
- sdf_skip_gain: bfloat16 [256], P(('fsdp', 'rep')), may hold values from 0.5 to 2
- sdf_skip_bias: bfloat16 [256], P(('fsdp', 'rep')), may hold values from -1.5 to 1.5
- sdf_last_dir: bfloat16 [256, 257], P(('fsdp', 'rep')), may hold values from -0.375 to 0.375
- sdf_last_gain: bfloat16 [257], replicated, may hold values from 0.5 to 2
- sdf_last_bias: bfloat16 [257], replicated, may hold values from -1.5 to 1.5
- color_first_dir: bfloat16 [289, 256], P(None, ('fsdp', 'rep')), may hold values from -0.375 to 0.375
- color_first_gain: bfloat16 [256], P(('fsdp', 'rep')), may hold values from 0.5 to 2
- color_first_bias: bfloat16 [256], P(('fsdp', 'rep')), may hold values from -1.5 to 1.5
- color_mid_dir: bfloat16 [3, 256, 256], P(None, None, ('fsdp', 'rep')), may hold values from -0.375 to 0.375
- color_mid_gain: bfloat16 [3, 256], P(None, ('fsdp', 'rep')), may hold values from 0.5 to 2
- color_mid_bias: bfloat16 [3, 256], P(None, ('fsdp', 'rep')), may hold values from -1.5 to 1.5
- color_last_dir: bfloat16 [256, 3], P(('fsdp', 'rep')), may hold values from -0.375 to 0.375
- color_last_gain: bfloat16 [3], replicated, may hold values from 0.5 to 2
- color_last_bias: bfloat16 [3], replicated, may hold values from -1.5 to 1.5
- variance: float32 [1], replicated, may hold values from 0.05 to 0.15
- rgb_cotangent: float32 [3, 1024], P(None, ('fsdp', 'rep')), may hold values from -6 to 6
Outputs:
- rgb: float32 [3, 1024], P(None, ('fsdp', 'rep'))
- anchors_grad: float32 [3, 1024], P(None, ('fsdp', 'rep'))
- directions_grad: float32 [3, 1024], P(None, ('fsdp', 'rep'))
- deltas_grad: float32 [1024, 128], P(('fsdp', 'rep'))
- sdf_first_dir_grad: float32 [39, 256], P(None, ('fsdp', 'rep'))
- sdf_first_gain_grad: float32 [256], P(('fsdp', 'rep'))
- sdf_first_bias_grad: float32 [256], P(('fsdp', 'rep'))
- sdf_mid_dir_grad: float32 [4, 256, 256], P(None, None, ('fsdp', 'rep'))
- sdf_mid_gain_grad: float32 [4, 256], P(None, ('fsdp', 'rep'))
- sdf_mid_bias_grad: float32 [4, 256], P(None, ('fsdp', 'rep'))
- sdf_narrow_dir_grad: float32 [256, 217], P(('fsdp', 'rep'))
- sdf_narrow_gain_grad: float32 [217], replicated
- sdf_narrow_bias_grad: float32 [217], replicated
- sdf_skip_dir_grad: float32 [256, 256], P(None, ('fsdp', 'rep'))
- sdf_skip_gain_grad: float32 [256], P(('fsdp', 'rep'))
- sdf_skip_bias_grad: float32 [256], P(('fsdp', 'rep'))
- sdf_last_dir_grad: float32 [256, 257], P(('fsdp', 'rep'))
- sdf_last_gain_grad: float32 [257], replicated
- sdf_last_bias_grad: float32 [257], replicated
- color_first_dir_grad: float32 [289, 256], P(None, ('fsdp', 'rep'))
- color_first_gain_grad: float32 [256], P(('fsdp', 'rep'))
- color_first_bias_grad: float32 [256], P(('fsdp', 'rep'))
- color_mid_dir_grad: float32 [3, 256, 256], P(None, None, ('fsdp', 'rep'))
- color_mid_gain_grad: float32 [3, 256], P(None, ('fsdp', 'rep'))
- color_mid_bias_grad: float32 [3, 256], P(None, ('fsdp', 'rep'))
- color_last_dir_grad: float32 [256, 3], P(('fsdp', 'rep'))
- color_last_gain_grad: float32 [3], replicated
- color_last_bias_grad: float32 [3], replicated
- variance_grad: float32 [1], replicated
The draws below stay inside these ranges and needn't reach their ends.
Inputs may be any that keep to these rules, and one draw needn't show every extreme that they name: The share of foreground samples differs from one device's 32 rays to another's; in every draw the rays of some device are foreground at every sample.
All inputs are finite; a program needn't handle non-finite values.
Results may differ from the reference program's by a relative error of at most 0.039.
The reference program's roundings to bfloat16 on the way count: a program that leaves them out, or rounds other values in their place, can miss the bound.
Values may be sent and summed in bfloat16 or wider, within the bound.
A program may use at most 320 MiB of HBM per device.

```python
import math
import jax
import jax.numpy as jnp
from jax import lax

H = 256
FREQ = 6
VFREQ = 4
SAMP = 128
RAY_DEV = 32
E = 39
NARROW = 217
OUTW = 257
CIN = 289
RAYS = 1024


def draw_foreground(key, part):
    key = jax.random.fold_in(key, 7)
    level_key, pick_key, gap_key, coin_key = jax.random.split(key, 4)
    blocks = RAYS // RAY_DEV
    levels = jax.random.randint(level_key, (blocks,), 1, 21)
    full_block = jax.random.randint(pick_key, (), 0, blocks)
    sparse_block = (full_block + 1 + jax.random.randint(gap_key, (), 0, blocks - 1)) % blocks
    block_ids = jnp.arange(blocks)
    levels = jnp.where(block_ids == full_block, 20, jnp.where(block_ids == sparse_block, 1, levels))
    per_ray = jnp.repeat(levels, RAY_DEV, total_repeat_length=RAYS)
    coin_draws = jax.random.randint(coin_key, (RAYS, SAMP), 0, 20)
    return (coin_draws < per_ray[:, None]).astype(jnp.int32)


def level_of(stream_key, extent, cuts, low, largest):
    def one(dim, parts):
        heights = jax.random.uniform(jax.random.fold_in(jax.random.fold_in(stream_key, 6), dim), (parts,), jnp.float32, low / len(cuts), largest / len(cuts))
        return jnp.repeat(jnp.exp(heights), extent[dim] // parts).reshape((-1,) + (1,) * (len(extent) - dim - 1))

    level = one(*cuts[0])
    for cut in cuts[1:]:
        level = level * one(*cut)
    return level


def scatter_about(stream_key, extent, scale, bound, cuts=(), kind=jnp.bfloat16):
    level = level_of(stream_key, extent, cuts, -0.22, 0.18) if cuts else 1.0
    values = jax.random.normal(stream_key, extent, jnp.float32) * scale * level
    return jnp.minimum(jnp.maximum(values, -bound), bound).astype(kind)


def setup_inputs(seed: int = 0) -> dict:
    streams_of = jax.random.split(jax.random.key(seed), 31)
    anchors = scatter_about(streams_of[0], (3, RAYS), 0.3, 4.0, ((1, 32),), jnp.float32)
    directions = scatter_about(streams_of[1], (3, RAYS), 0.6, 4.0, ((1, 32),), jnp.float32)
    deltas = jnp.clip(jnp.exp(math.log(0.1) - 1.609438 * jax.random.uniform(streams_of[2], (RAYS, SAMP), jnp.float32) ** level_of(streams_of[2], (RAYS, SAMP), ((0, 32),), -0.2, 0.2)), 0.02, 0.1)
    foreground = draw_foreground(jax.random.fold_in(streams_of[30], 71), 0)
    sdf_first_dir = scatter_about(streams_of[4], (E, H), E ** -0.5, 1.0, ((1, 32),))
    sdf_first_gain = jnp.clip(jnp.exp(math.log(2.0) - 1.3862944 * jax.random.uniform(streams_of[5], (H,), jnp.float32) ** level_of(streams_of[5], (H,), ((0, 32),), -0.2, 0.2)), 0.5, 2.0).astype(jnp.bfloat16)
    sdf_first_bias = scatter_about(streams_of[6], (H,), 0.3, 1.5, ((0, 32),))
    sdf_mid_dir = scatter_about(streams_of[7], (4, H, H), H ** -0.5, 0.375, ((2, 32),))
    sdf_mid_gain = jnp.clip(jnp.exp(math.log(2.0) - 1.3862944 * jax.random.uniform(streams_of[8], (4, H), jnp.float32) ** level_of(streams_of[8], (4, H), ((1, 32),), -0.2, 0.2)), 0.5, 2.0).astype(jnp.bfloat16)
    sdf_mid_bias = scatter_about(streams_of[9], (4, H), 0.3, 1.5, ((1, 32),))
    sdf_narrow_dir = scatter_about(streams_of[10], (H, NARROW), H ** -0.5, 0.375, ((0, 32),))
    sdf_narrow_gain = jnp.clip(jnp.exp(jax.random.uniform(streams_of[11], (NARROW,), jnp.float32, math.log(0.5), math.log(2.0))), 0.5, 2.0).astype(jnp.bfloat16)
    sdf_narrow_bias = scatter_about(streams_of[12], (NARROW,), 0.3, 1.5)
    sdf_skip_dir = scatter_about(streams_of[13], (H, H), H ** -0.5, 0.375, ((1, 32),))
    sdf_skip_gain = jnp.clip(jnp.exp(math.log(2.0) - 1.3862944 * jax.random.uniform(streams_of[14], (H,), jnp.float32) ** level_of(streams_of[14], (H,), ((0, 32),), -0.2, 0.2)), 0.5, 2.0).astype(jnp.bfloat16)
    sdf_skip_bias = scatter_about(streams_of[15], (H,), 0.3, 1.5, ((0, 32),))
    sdf_last_dir = scatter_about(streams_of[16], (H, OUTW), H ** -0.5, 0.375, ((0, 32),))
    sdf_last_gain = jnp.clip(jnp.exp(jax.random.uniform(streams_of[17], (OUTW,), jnp.float32, math.log(0.5), math.log(2.0))), 0.5, 2.0).astype(jnp.bfloat16)
    sdf_last_bias = scatter_about(streams_of[18], (OUTW,), 0.3, 1.5)
    color_first_dir = scatter_about(streams_of[19], (CIN, H), CIN ** -0.5, 0.375, ((1, 32),))
    color_first_gain = jnp.clip(jnp.exp(math.log(2.0) - 1.3862944 * jax.random.uniform(streams_of[20], (H,), jnp.float32) ** level_of(streams_of[20], (H,), ((0, 32),), -0.2, 0.2)), 0.5, 2.0).astype(jnp.bfloat16)
    color_first_bias = scatter_about(streams_of[21], (H,), 0.3, 1.5, ((0, 32),))
    color_mid_dir = scatter_about(streams_of[22], (3, H, H), H ** -0.5, 0.375, ((2, 32),))
    color_mid_gain = jnp.clip(jnp.exp(math.log(2.0) - 1.3862944 * jax.random.uniform(streams_of[23], (3, H), jnp.float32) ** level_of(streams_of[23], (3, H), ((1, 32),), -0.2, 0.2)), 0.5, 2.0).astype(jnp.bfloat16)
    color_mid_bias = scatter_about(streams_of[24], (3, H), 0.3, 1.5, ((1, 32),))
    color_last_dir = scatter_about(streams_of[25], (H, 3), H ** -0.5, 0.375, ((0, 32),))
    color_last_gain = jnp.clip(jnp.exp(jax.random.uniform(streams_of[26], (3,), jnp.float32, math.log(0.5), math.log(2.0))), 0.5, 2.0).astype(jnp.bfloat16)
    color_last_bias = scatter_about(streams_of[27], (3,), 0.3, 1.5)
    variance = jnp.clip(jax.random.uniform(streams_of[28], (1,), jnp.float32, 0.05, 0.15), 0.05, 0.15)
    rgb_cotangent = scatter_about(streams_of[29], (3, RAYS), 1.0, 6.0, ((1, 32),), jnp.float32)
    return {"anchors": anchors, "directions": directions, "deltas": deltas, "foreground": foreground, "sdf_first_dir": sdf_first_dir, "sdf_first_gain": sdf_first_gain, "sdf_first_bias": sdf_first_bias, "sdf_mid_dir": sdf_mid_dir, "sdf_mid_gain": sdf_mid_gain, "sdf_mid_bias": sdf_mid_bias, "sdf_narrow_dir": sdf_narrow_dir, "sdf_narrow_gain": sdf_narrow_gain, "sdf_narrow_bias": sdf_narrow_bias, "sdf_skip_dir": sdf_skip_dir, "sdf_skip_gain": sdf_skip_gain, "sdf_skip_bias": sdf_skip_bias, "sdf_last_dir": sdf_last_dir, "sdf_last_gain": sdf_last_gain, "sdf_last_bias": sdf_last_bias, "color_first_dir": color_first_dir, "color_first_gain": color_first_gain, "color_first_bias": color_first_bias, "color_mid_dir": color_mid_dir, "color_mid_gain": color_mid_gain, "color_mid_bias": color_mid_bias, "color_last_dir": color_last_dir, "color_last_gain": color_last_gain, "color_last_bias": color_last_bias, "variance": variance, "rgb_cotangent": rgb_cotangent}


eps_norm = 1e-06
near_plane = 0.1
root_half = 0.7071067811865476

@jax.custom_vjp
def low(v):
    return lax.optimization_barrier(v.astype(jnp.bfloat16)).astype(jnp.float32)

@jax.custom_vjp
def low_back(v):
    return v

def low_keep(v):
    return (low(v), None)

def low_pass(kept, grad):
    return (grad,)

def back_keep(v):
    return (v, None)

def back_low(kept, grad):
    return (low(grad),)
low.defvjp(low_keep, low_pass)
low_back.defvjp(back_keep, back_low)

def rounded(values):
    return low(low_back(values))

def project(rows, weight, offset):
    return jnp.dot(rounded(rows), rounded(weight), precision=lax.Precision.HIGHEST) + offset

def scaled(direction, column_gain):
    return direction * (column_gain * lax.rsqrt(lax.optimization_barrier(jnp.sum(direction * direction, axis=0)) + eps_norm))

def sharp(values):
    return jax.nn.softplus(2.0 * values) / 2.0

def encode(points, repeats):
    pieces = [points]
    for octave in range(repeats):
        pieces.append(jnp.sin(points * 2.0 ** octave))
        pieces.append(jnp.cos(points * 2.0 ** octave))
    return jnp.concatenate(pieces, axis=1)

def sdf_net(params, points):
    first_dir, first_gain, first_bias, mid_dir, mid_gain, mid_bias = params[0:6]
    narrow_dir, narrow_gain, narrow_bias, skip_dir, skip_gain, skip_bias = params[6:12]
    last_dir, last_gain, last_bias = params[12:15]
    encoded = encode(points, FREQ)
    hidden = sharp(project(encoded, scaled(first_dir, first_gain), first_bias))
    for section in range(2):
        hidden = sharp(project(hidden, scaled(mid_dir[section], mid_gain[section]), mid_bias[section]))
    hidden = sharp(project(hidden, scaled(narrow_dir, narrow_gain), narrow_bias))
    hidden = jnp.concatenate([hidden, encoded], axis=1) * root_half
    hidden = sharp(project(hidden, scaled(skip_dir, skip_gain), skip_bias))
    for section in range(2, 4):
        hidden = sharp(project(hidden, scaled(mid_dir[section], mid_gain[section]), mid_bias[section]))
    output = project(hidden, scaled(last_dir, last_gain), last_bias)
    return (output[:, 0], output[:, 1:])

def color_net(params, points, viewing, normal, features):
    first_dir, first_gain, first_bias, mid_dir, mid_gain, mid_bias = params[15:21]
    last_dir, last_gain, last_bias = params[21:24]
    joined = jnp.concatenate([points, encode(viewing, VFREQ), normal, features], axis=1)
    hidden = jax.nn.silu(project(joined, scaled(first_dir, first_gain), first_bias))
    for section in range(3):
        hidden = jax.nn.silu(project(hidden, scaled(mid_dir[section], mid_gain[section]), mid_bias[section]))
    return jax.nn.sigmoid(project(hidden, scaled(last_dir, last_gain), last_bias))

def render(params, anchors, directions, deltas, foreground):
    anchor_rows = anchors.T
    direction_rows = directions.T
    ray_count, sample_count = deltas.shape
    depths = near_plane + jnp.cumsum(deltas, axis=1) - 0.5 * deltas
    points = (anchor_rows[:, None, :] + depths[:, :, None] * direction_rows[:, None, :]).reshape(ray_count * sample_count, 3)
    viewing = jnp.broadcast_to(direction_rows[:, None, :], (ray_count, sample_count, 3)).reshape(ray_count * sample_count, 3)

    def sdf_total(moved):
        signed, features = sdf_net(params, moved)
        return (jnp.sum(signed), (signed, features))
    normal, (signed, features) = jax.grad(sdf_total, has_aux=True)(points)
    colors = color_net(params, points, viewing, normal, features).reshape(ray_count, sample_count, 3)
    cosine = lax.optimization_barrier(jnp.sum(viewing * normal, axis=1))
    slope_term = -jax.nn.softplus(-10.0 * cosine) / 10.0
    halfway = slope_term * deltas.reshape(-1) * 0.5
    inverse_s = jnp.exp(10.0 * params[24][0])
    before = jax.nn.sigmoid((signed - halfway) * inverse_s)
    after = jax.nn.sigmoid((signed + halfway) * inverse_s)
    ratio = (before - after + 1e-05) / (before + 1e-05)
    opacity = (jax.nn.softplus(20.0 * ratio) - jax.nn.softplus(20.0 * (ratio - 1.0))) / 20.0
    opacity = foreground * opacity.reshape(ray_count, sample_count)
    survive = jnp.cumprod(1.0 - opacity + 1e-07, axis=1)
    through = jnp.concatenate([jnp.ones((ray_count, 1), jnp.float32), survive[:, :-1]], axis=1)
    contrib = opacity * through
    return lax.optimization_barrier(jnp.sum(contrib[:, :, None] * colors, axis=1)).T

def reference(anchors, directions, deltas, foreground, sdf_first_dir, sdf_first_gain, sdf_first_bias, sdf_mid_dir, sdf_mid_gain, sdf_mid_bias, sdf_narrow_dir, sdf_narrow_gain, sdf_narrow_bias, sdf_skip_dir, sdf_skip_gain, sdf_skip_bias, sdf_last_dir, sdf_last_gain, sdf_last_bias, color_first_dir, color_first_gain, color_first_bias, color_mid_dir, color_mid_gain, color_mid_bias, color_last_dir, color_last_gain, color_last_bias, variance, rgb_cotangent):
    weights = (sdf_first_dir, sdf_first_gain, sdf_first_bias, sdf_mid_dir, sdf_mid_gain, sdf_mid_bias, sdf_narrow_dir, sdf_narrow_gain, sdf_narrow_bias, sdf_skip_dir, sdf_skip_gain, sdf_skip_bias, sdf_last_dir, sdf_last_gain, sdf_last_bias, color_first_dir, color_first_gain, color_first_bias, color_mid_dir, color_mid_gain, color_mid_bias, color_last_dir, color_last_gain, color_last_bias, variance)
    params = tuple((entry.astype(jnp.float32) for entry in weights))
    anchors = anchors.astype(jnp.float32)
    directions = directions.astype(jnp.float32)
    deltas = deltas.astype(jnp.float32)
    fore_float = foreground.astype(jnp.float32)
    blocks = anchors.shape[1] // RAY_DEV

    def forward(params, anchors, directions, deltas):

        def per_block(items):
            return render(params, items[0], items[1], items[2], items[3])
        anchor_blocks = anchors.reshape(3, blocks, RAY_DEV).transpose(1, 0, 2)
        direction_blocks = directions.reshape(3, blocks, RAY_DEV).transpose(1, 0, 2)
        delta_blocks = deltas.reshape(blocks, RAY_DEV, deltas.shape[1])
        fore_blocks = fore_float.reshape(blocks, RAY_DEV, deltas.shape[1])
        colors = lax.map(jax.checkpoint(per_block), (anchor_blocks, direction_blocks, delta_blocks, fore_blocks))
        return colors.transpose(1, 0, 2).reshape(3, blocks * RAY_DEV)
    rgb, pullback = jax.vjp(forward, params, anchors, directions, deltas)
    grads, anchors_grad, directions_grad, deltas_grad = pullback(rgb_cotangent.astype(rgb.dtype))
    return (rgb, anchors_grad, directions_grad, deltas_grad, grads[0], grads[1], grads[2], grads[3], grads[4], grads[5], grads[6], grads[7], grads[8], grads[9], grads[10], grads[11], grads[12], grads[13], grads[14], grads[15], grads[16], grads[17], grads[18], grads[19], grads[20], grads[21], grads[22], grads[23], grads[24])
```

```python
import functools

import jax
import jax.numpy as jnp
from jax import lax
from jax.experimental import pallas as pl
from jax.experimental.pallas import tpu as pltpu
from jax.sharding import PartitionSpec as P

F32 = jnp.float32
BF = jnp.bfloat16
H = 256
SAMP = 128
ENC = 39
EROWS = 48
NARROW = 217
NX = 33
GROUPS = 12
SUB = 256
RC = 8
PTS = RC * SAMP
NSUB = PTS // SUB
RSUB = SUB // SAMP
CROSS = 128
BIASES = 200
TAIL = 216
EPS = 1e-06
HALF_LN2 = 0.34657359027997264
ROOT_HALF = 0.7071067811865476


def nn(a, b):
    return lax.dot_general(a, b, (((1,), (0,)), ((), ())), preferred_element_type=F32)


def nt(a, b):
    return lax.dot_general(a, b, (((1,), (1,)), ((), ())), preferred_element_type=F32)


def exact(a, b):
    return lax.dot_general(
        a, b, (((1,), (0,)), ((), ())), precision=lax.Precision.HIGHEST, preferred_element_type=F32
    )


def iota(shape, dim):
    return lax.broadcasted_iota(jnp.int32, shape, dim)


def column(row):
    n = row.shape[1]
    return jnp.sum(jnp.where(iota((n, n), 0) == iota((n, n), 1), row, 0.0), axis=1, keepdims=True)


def as_row(ref):
    return ref[...].astype(F32).reshape(1, ref.shape[0])


def line(col):
    n = col.shape[0]
    return jnp.sum(jnp.where(iota((n, n), 0) == iota((n, n), 1), col, 0.0), axis=0, keepdims=True)


def wide(half):
    return jnp.concatenate([half, half], axis=1)


def sharp(z):
    z = z.astype(BF)
    s = 0.5 * jnp.tanh(z) + 0.5
    return jnp.maximum(z, 0.0) - 0.5 * jnp.log(jnp.maximum(s, 1.0 - s)), s


def silu(z):
    z = z.astype(BF)
    g = 0.5 * jnp.tanh(0.5 * z) + 0.5
    h = z * g
    return h, g + h * (1.0 - g)


def softplus(x):
    return jnp.maximum(x, 0.0) + jnp.log(1.0 + jnp.exp(-jnp.abs(x)))


def sigmoid(x):
    return 1.0 / (1.0 + jnp.exp(-x))


def scaled_rows(d, gain):
    return d * (gain * lax.rsqrt(jnp.sum(d * d, axis=1, keepdims=True) + EPS))


def share_rows(first, narrow, last, cfirst, wid):
    r = first.shape[0]

    def padded(k, ref, lanes):
        wid[k] = jnp.zeros(wid.shape[1:], F32)
        wid[k, :, 0 : ref.shape[1]] = ref[...].astype(F32)
        return wid[k][:, 0:lanes]

    return (padded(0, first, 128), padded(1, narrow, H), padded(2, last, 384), padded(3, cfirst, 384))


class Place:
    def __init__(self, fsdp):
        f, p = lax.axis_index("fsdp"), lax.axis_index("rep")
        self.depth = fsdp // 2
        self.z, self.y, self.x, self.c = f // 2, f % 2, p // 2, p % 2

    def at(self, half, z, a=0, b=0, c=0):
        dy, dx = (a, b) if half == 0 else (b, a)
        return z, (self.y + dy) % 2, (self.x + dx) % 2, (self.c + c) % 2

    def index(self, *where):
        z, y, x, c = self.at(*where)
        return ((z * 2 + y) * 2 + x) * 2 + c

    def device(self, *where):
        z, y, x, c = self.at(*where)
        return z * 2 + y, x * 2 + c

    def turn(self, k):
        return (self.z + k) % self.depth

    def greet(self, barrier):
        def one(k, carry):
            signal(barrier, self.device(0, self.turn(k)))
            return carry

        lax.fori_loop(1, self.depth, one, 0)
        for flips in ((1, 0, 0), (0, 1, 0), (0, 0, 1)):
            signal(barrier, self.device(0, self.z, *flips))

    def wait_all(self, barrier):
        pl.semaphore_wait(barrier, self.depth + 2)


def signal(sem, device):
    pl.semaphore_signal(sem, inc=1, device_id=device, device_id_type=pl.DeviceIdType.MESH)


def remote(src, dst, send, recv, device):
    return pltpu.make_async_remote_copy(
        src_ref=src, dst_ref=dst, send_sem=send, recv_sem=recv,
        device_id=device, device_id_type=pl.DeviceIdType.MESH,
    )


def each(start, stop, body):
    def one(k, carry):
        body(k)
        return carry

    lax.fori_loop(start, stop, one, 0)


def own_share(
    first, mid, narrow, skip, last, cfirst, cmid, fg, fb, mg, mb, sg, sb, cg, cb, cmg, cmb, cl, wid
):
    d_first, d_narrow, d_last, d_cfirst = share_rows(first, narrow, last, cfirst, wid)

    def vec(ref, k=None):
        row = as_row(ref) if k is None else ref[...].astype(F32)[k : k + 1]
        return column(row)

    lane = iota((1, 128), 1)
    parts = [scaled_rows(mid[k].astype(F32), vec(mg, k)) for k in range(4)]
    parts.append(pltpu.roll(scaled_rows(skip[...].astype(F32), vec(sg)), ENC, 1))
    parts += [scaled_rows(cmid[k].astype(F32), vec(cmg, k)) for k in range(3)]
    s_cfirst = scaled_rows(d_cfirst, vec(cg))
    parts.append(pltpu.roll(s_cfirst, 384 - NX, 1)[:, 0:H])
    left = scaled_rows(d_first, vec(fg)) + jnp.where(lane == ENC, vec(fb), 0.0)
    right = jnp.where(lane < NX, s_cfirst[:, 0:128], 0.0) + jnp.where(lane == NX, vec(cb), 0.0)
    biases = [(1, mb, 0), (2, mb, 1), (3, mb, 2), (4, mb, 3), (5, sb, None), (7, cmb, 0), (8, cmb, 1), (9, cmb, 2)]
    for j, ref, k in biases:
        right = right + jnp.where(lane == BIASES - 128 + j, vec(ref, k), 0.0)
    right = right + jnp.where(lane == TAIL - 128, d_last[:, 0:1], 0.0)
    for c in range(3):
        right = right + jnp.where(lane == TAIL - 127 + c, vec(cl, c), 0.0)
    parts.append(jnp.concatenate([left, right], axis=1))
    parts.append(pltpu.roll(d_narrow, ENC, 1))
    parts.append(pltpu.roll(d_last, 383, 1)[:, 0:H])
    return jnp.concatenate(parts, axis=0).astype(BF)


def gather(place, out, send, recv, meanwhile):
    z, depth = place.z, place.depth
    me = place.index(0, z)
    rows = out.shape[1] // 2

    def copy(half, slab, s, *to):
        part = out.at[slab, pl.ds(half * rows, rows)]
        return remote(part, part, send.at[half, s], recv.at[half, slab], place.device(half, *to))

    def arrived(half, slab):
        copy(half, slab, 0, z, 0, 0, 1).wait_recv()

    def along_z(k):
        for half in range(2):
            copy(half, me, k - 1, place.turn(k)).start()

    def pass_on(half, slab, t, stage):
        base = depth - 1
        if stage == 0:
            copy(half, slab, base + t, z, 1).start()
        if stage <= 1:
            copy(half, slab, base + depth + 2 * t + stage, z, 0, 1).start()
        copy(half, slab, base + 3 * depth + 4 * t + stage, z, 0, 0, 1).start()

    each(1, depth, along_z)
    for half in range(2):
        pass_on(half, me, 0, 0)

    def from_z(k):
        for half in range(2):
            slab = place.index(half, place.turn(k))
            arrived(half, slab)
            pass_on(half, slab, k, 0)

    def from_a(k):
        for half in range(2):
            slab = place.index(half, place.turn(k), 1)
            arrived(half, slab)
            pass_on(half, slab, k, 1)

    def from_b(k):
        for half in range(2):
            slab = place.index(half, place.turn(k), 0, 1)
            arrived(half, slab)
            pass_on(half, slab, k, 2)

    def from_ab(k):
        for half in range(2):
            slab = place.index(half, place.turn(k), 1, 1)
            arrived(half, slab)
            pass_on(half, slab, k, 3)

    def from_core(k):
        for half in range(2):
            for a in range(2):
                for b in range(2):
                    arrived(half, place.index(half, place.turn(k), a, b, 1))

    def sent(s):
        for half in range(2):
            copy(half, me, s, z, 0, 0, 1).wait_send()

    meanwhile()
    each(1, depth, from_z)
    each(0, depth, from_a)
    each(0, depth, from_b)
    each(0, depth, from_ab)
    each(0, depth, from_core)
    each(0, 8 * depth - 1, sent)


def compute_kernel(
    fsdp, anch, dirs, delt, fore, cot, var, ng, nb, lg, lb, cg, cb, *rest
):
    layers, rest = rest[:18], rest[18:]
    compute_body(fsdp, layers, anch, dirs, delt, fore, cot, var, ng, nb, lg, lb, cg, cb, *rest)


def compute_body(
    fsdp, layers, anch, dirs, delt, fore, cot, var, ng, nb, lg, lb, cg, cb,
    rgb_o, ag_o, dg_o, deltag_o, gout, tot_o, inv_o, smalls,
    gathered, wid, send, recv, wts, sm, wt, w, wt7, w0t, w0, wcft, wcx, wclt, wcl, w7s, bb,
    enc, fe, xt, dep, cols,
    hx, ss, us, zg, ts, fx, hc, dc, zc, encb, dzb,
    de, nr, row7, rowc, dzr, dx, eb, outc,
    acc, acc0, accx, accl, vac,
):
    rays = delt.shape[0]
    lane128 = iota((1, 128), 1)

    place = Place(fsdp)
    barrier = pltpu.get_barrier_semaphore()
    place.greet(barrier)
    gathered[place.index(0, place.z)] = own_share(*layers, wid)
    place.wait_all(barrier)

    def meanwhile():
        cols[...] = jnp.zeros(cols.shape, F32)
        cols[0:3, 0:rays] = anch[...]
        cols[3:6, 0:rays] = dirs[...]
        cols[6:9, 0:rays] = cot[...]
        percol = cols[...].T
        cols[...] = percol
        low = (iota((SAMP, SAMP), 0) <= iota((SAMP, SAMP), 1)).astype(F32)
        dall = delt[...]
        depth = 0.1 + exact(dall, low) - 0.5 * dall
        dep[...] = depth
        enc[...] = jnp.zeros(enc.shape, F32)
        xt[...] = jnp.zeros(xt.shape, F32)
        enc[pl.ds(ENC, rays, stride=EROWS), :] = jnp.ones((rays, SAMP), F32)
        xt[pl.ds(NX, rays, stride=EROWS), :] = jnp.ones((rays, SAMP), F32)

        def put_enc(f, value):
            fe[f] = value
            enc[pl.ds(f, rays, stride=EROWS), :] = value

        for c in range(3):
            view = jnp.broadcast_to(percol[0:rays, 3 + c : 4 + c], (rays, SAMP))
            p = percol[0:rays, c : c + 1] + depth * view
            put_enc(c, p)
            xt[pl.ds(c, rays, stride=EROWS), :] = p
            sn, cs = jnp.sin(p), jnp.cos(p)
            for k in range(6):
                put_enc(3 + 6 * k + c, sn)
                put_enc(6 + 6 * k + c, cs)
                sn, cs = 2.0 * sn * cs, 1.0 - 2.0 * sn * sn
            xt[pl.ds(3 + c, rays, stride=EROWS), :] = view
            sn, cs = jnp.sin(view), jnp.cos(view)
            for k in range(4):
                xt[pl.ds(6 + 6 * k + c, rays, stride=EROWS), :] = sn
                xt[pl.ds(9 + 6 * k + c, rays, stride=EROWS), :] = cs
                sn, cs = 2.0 * sn * cs, 1.0 - 2.0 * sn * sn

        nr[...] = jnp.zeros(nr.shape, F32)
        eb[...] = jnp.zeros(eb.shape, F32)
        dzr[...] = jnp.zeros(dzr.shape, F32)
        acc[...] = jnp.zeros(acc.shape, F32)
        acc0[...] = jnp.zeros(acc0.shape, F32)
        accx[...] = jnp.zeros(accx.shape, F32)
        accl[...] = jnp.zeros(accl.shape, F32)
        vac[...] = jnp.zeros(vac.shape, F32)
        hx[:, H : H + 16, 0:PTS] = jnp.ones((7, 16, PTS), BF)
        hx[:, H : H + 16, PTS:] = jnp.zeros((7, 16, PTS), BF)
        dzb[:, PTS:] = jnp.where(iota((16, PTS), 0) == 0, 1.0, 0.0).astype(BF)
        hc[:, H : H + 16, :] = jnp.ones((4, 16, PTS), BF)

    gather(place, gathered, send, recv, meanwhile)

    lane256 = iota((1, H), 1)
    sm[...] = jnp.zeros(sm.shape, F32)
    for k, ref in enumerate((ng, nb, lg, lb, cg, cb)):
        sm[k : k + 1, 0 : ref.shape[0]] = as_row(ref)
    near = pltpu.roll(sm[:, 0:H], H - NARROW, 1)
    tail_row = []
    for k in (0, 1):
        t = jnp.where(lane256 == TAIL, sm[2 + k : 3 + k, 0:1], 0.0)
        for c in range(3):
            t = t + jnp.where(lane256 == TAIL + 1 + c, sm[4 + k : 5 + k, c : c + 1], 0.0)
        tail_row.append(t)
    smalls[...] = jnp.concatenate(
        [
            near[0:1],
            near[1:2] + jnp.where(lane256 < ENC, -1e4, 0.0),
            pltpu.roll(sm[...], 383, 1)[2:4, 0:H],
            tail_row[0],
            tail_row[1],
            jnp.broadcast_to(as_row(var), (1, H)),
            jnp.zeros((1, H), F32),
        ],
        axis=0,
    )
    r = H // gathered.shape[0]
    rp = gathered.shape[1] // GROUPS
    for q in range(GROUPS // 2):
        pair = gathered[:, 2 * rp * q : 2 * rp * (q + 1), :].astype(F32)
        wts[2 * q] = pair[:, 0:r].reshape(H, H).astype(BF)
        wts[2 * q + 1] = pair[:, rp : rp + r].reshape(H, H).astype(BF)

    unit = (iota((H, H), 0) == iota((H, H), 1)).astype(BF)

    def turned(x):
        return nt(unit, x)

    misc = wts[9].astype(F32)
    misct = turned(wts[9])
    for k, src in enumerate((0, 1, None, 4, 2, 3, 5, 6, 7)):
        if src is not None:
            wt[k] = wts[src]
            w[k] = turned(wts[src]).astype(BF)
    d3 = wts[10].astype(F32)
    inv3 = lax.rsqrt(jnp.sum(d3 * d3, axis=0, keepdims=True) + EPS)
    w3 = (d3 * (smalls[0:1, :] * inv3)).astype(BF)
    w[2] = w3
    wt[2] = turned(w3).astype(BF)
    d7 = wts[11].astype(F32)
    inv7 = lax.rsqrt(jnp.sum(d7 * d7, axis=0, keepdims=True) + EPS)
    w7 = (d7 * (smalls[2:3, :] * inv7)).astype(BF)
    w[9] = w7
    wt7[0:H] = turned(w7).astype(BF)
    w[10] = turned(wts[8]).astype(BF)
    invm = lax.rsqrt(jnp.sum(misc * misc, axis=0, keepdims=True) + EPS)
    tail = (misc * (smalls[4:5, :] * invm)).astype(BF)
    tailt = turned(tail)[TAIL : TAIL + 8]
    tail = tail.astype(F32)
    row8 = iota((8, H), 0)
    none8 = jnp.zeros((8, H), F32)
    wt7[H : H + 16] = jnp.concatenate([jnp.where(row8 == 0, tailt, 0.0), none8], axis=0).astype(BF)
    wclt[...] = jnp.concatenate(
        [jnp.where((row8 > 0) & (row8 < 4), tailt, 0.0), none8], axis=0
    ).astype(BF)
    only = jnp.where((lane256 > TAIL) & (lane256 < TAIL + 4), tail, 0.0)
    wcl[...] = pltpu.roll(only, H - TAIL, 1)[:, 0:16].astype(BF)
    w7s[...] = jnp.broadcast_to(tail[:, TAIL : TAIL + 1], (H, 128))
    w0t[...] = misc[:, 0:EROWS].astype(BF)
    w0[...] = misct[0:EROWS].astype(BF)
    wcx[...] = misct[CROSS : CROSS + EROWS].astype(BF)
    wcft[:, 0:H] = wts[8]
    wcft[:, H : H + EROWS] = misc[:, CROSS : CROSS + EROWS].astype(BF)
    for k, j in enumerate((1, 2, None, 5, 3, 4, None, 7, 8, 9)):
        if j is not None:
            bb[k] = jnp.broadcast_to(misc[:, BIASES + j : BIASES + j + 1], (H, 128))
    bb[2] = jnp.broadcast_to(column(smalls[1:2, :]), (H, 128))
    bb[6] = jnp.broadcast_to(column(smalls[3:4, :]), (H, 128))
    inv_o[...] = jnp.concatenate([inv3, inv3, inv7, inv7, invm, invm, invm, invm], axis=0)

    inv_s = jnp.exp(10.0 * smalls[6:7, 0:1])

    def chunk(i, carry):
        r0 = pl.multiple_of(i * RC, RC)
        e0 = pl.multiple_of(i * (RC * EROWS), 8)

        def sub(j):
            return slice(j * SUB, (j + 1) * SUB)

        def sub2(j):
            return slice(PTS + j * SUB, PTS + (j + 1) * SUB)

        def gather_rows(ref, base, j, count):
            start = base + j * RSUB * count
            if not isinstance(start, int):
                start = pl.multiple_of(start, 8)
                return jnp.concatenate(
                    [ref[pl.ds(pl.multiple_of(start + t * count, 8), count), :] for t in range(RSUB)],
                    axis=1,
                )
            return jnp.concatenate(
                [ref[start + t * count : start + (t + 1) * count, :] for t in range(RSUB)], axis=1
            )

        def spread_rows(ref, j, count, value):
            for t in range(RSUB):
                at = (j * RSUB + t) * count
                ref[at : at + count, :] = value[0:count, t * SAMP : (t + 1) * SAMP]

        def ray_row(ref, f, count):
            return ref[pl.ds(f, RC, stride=count), :]

        for j in range(NSUB):
            encb[:, sub(j)] = gather_rows(enc, e0, j, EROWS).astype(BF)
        for l in range(7):
            if l == 0:
                zz = nn(w0t[...], encb[:, 0:PTS])
            else:
                zz = nn(wt[l - 1], hx[l - 1, 0:H, 0:PTS])
            for j in range(NSUB):
                z = zz[:, sub(j)]
                if l > 0:
                    z = z + wide(bb[l - 1])
                h, s = sharp(z)
                ss[l, :, sub(j)] = s.astype(BF)
                if l == 3:
                    e = gather_rows(enc, e0, j, EROWS)
                    keep = iota((EROWS, 1), 0) < ENC
                    h = h.astype(F32)
                    h = ROOT_HALF * jnp.concatenate(
                        [h[0:EROWS] + jnp.where(keep, e, 0.0), h[EROWS:]], axis=0
                    )
                hx[l, 0:H, sub(j)] = h.astype(BF)
        zz = nn(wt7[...], hx[6, 0:H, 0:PTS])
        for j in range(NSUB):
            z = zz[:, sub(j)]
            fx[0:H, sub(j)] = (z[0:H] + wide(bb[6])).astype(BF)
            spread_rows(row7, j, 16, z[H : H + 16])

        for j in range(NSUB):
            zg[6, :, sub2(j)] = wide(w7s[...]).astype(BF) * ss[6, :, sub(j)]
        for l in range(6, 0, -1):
            uu = nn(w[l - 1], zg[l, :, PTS:])
            for j in range(NSUB):
                u = uu[:, sub(j)].astype(BF)
                if l == 4:
                    u = u.astype(F32) * ROOT_HALF
                    spread_rows(de, j, EROWS, u)
                    u = u.astype(BF)
                us[l - 1, :, sub(j)] = u
                zg[l - 1, :, sub2(j)] = u * ss[l - 1, :, sub(j)]
        dd = nn(w0[...], zg[0, :, PTS:]).astype(BF).astype(F32)
        for j in range(NSUB):
            d = dd[:, sub(j)]
            spread_rows(de, j, EROWS, d + gather_rows(de, 0, j, EROWS))

        def feature(f):
            return fe[f, pl.ds(r0, RC), :]

        dcol = [percol_ref_col(cols, r0, 3 + c) for c in range(3)]
        ccol = [percol_ref_col(cols, r0, 6 + c) for c in range(3)]
        normal = []
        for c in range(3):
            n = ray_row(de, c, EROWS)
            for k in range(6):
                n = n + 2.0**k * (
                    feature(6 + 6 * k + c) * ray_row(de, 3 + 6 * k + c, EROWS)
                    - feature(3 + 6 * k + c) * ray_row(de, 6 + 6 * k + c, EROWS)
                )
            normal.append(n)
            nr[pl.ds(30 + c, RC, stride=EROWS), :] = n

        delta = delt[pl.ds(r0, RC), :]
        front = fore[pl.ds(r0, RC), :].astype(F32)
        signed = ray_row(row7, 0, 16) + smalls[5:6, TAIL : TAIL + 1]
        cosine = dcol[0] * normal[0] + dcol[1] * normal[1] + dcol[2] * normal[2]
        slope = softplus(-10.0 * cosine) * -0.1
        slope_d = sigmoid(-10.0 * cosine)
        half = slope * delta * 0.5
        before = sigmoid((signed - half) * inv_s)
        after = sigmoid((signed + half) * inv_s)
        ratio = (before - after + 1e-05) / (before + 1e-05)
        ratio_d = front * (sigmoid(20.0 * ratio) - sigmoid(20.0 * (ratio - 1.0)))
        opacity = front * (softplus(20.0 * ratio) - softplus(20.0 * (ratio - 1.0))) * 0.05
        factor = 1.0 - opacity + 1e-07
        survive = factor
        lane = iota((RC, SAMP), 1)
        step = 1
        while step < SAMP:
            survive = survive * jnp.where(lane >= step, pltpu.roll(survive, step, 1), 1.0)
            step *= 2
        through = jnp.where(lane >= 1, pltpu.roll(survive, 1, 1), 1.0)
        contrib = opacity * through

        for j in range(NSUB):
            x = gather_rows(xt, e0, j, EROWS) + gather_rows(nr, 0, j, EROWS)
            fx[H : H + EROWS, sub(j)] = x.astype(BF)
        for l in range(4):
            if l == 0:
                zz = nn(wcft[...], fx[...])
            else:
                zz = nn(wt[5 + l], hc[l - 1, 0:H])
            for j in range(NSUB):
                z = zz[:, sub(j)]
                if l > 0:
                    z = z + wide(bb[6 + l])
                h, d = silu(z)
                hc[l, 0:H, sub(j)] = h.astype(BF)
                dc[l, :, sub(j)] = d.astype(BF)
        zz = nn(wclt[...], hc[3, 0:H])
        for j in range(NSUB):
            spread_rows(rowc, j, 16, zz[:, sub(j)])

        out = jnp.zeros((RC, 128), F32)
        dcontrib = jnp.zeros((RC, SAMP), F32)
        for c in range(3):
            color = sigmoid(ray_row(rowc, 1 + c, 16) + smalls[5:6, TAIL + 1 + c : TAIL + 2 + c])
            out = out + jnp.where(lane128 == c, jnp.sum(contrib * color, axis=1, keepdims=True), 0.0)
            dcontrib = dcontrib + ccol[c] * color
            dlogit = ccol[c] * contrib * color * (1.0 - color)
            dzr[pl.ds(1 + c, RC, stride=16), :] = dlogit
            vac[2 + c] += dlogit
        weighted = dcontrib * contrib
        after_sum = exact(weighted, (iota((SAMP, SAMP), 0) > iota((SAMP, SAMP), 1)).astype(F32))
        dratio = (dcontrib * through - after_sum / factor) * ratio_d
        base = 1.0 / (before + 1e-05)
        dbefore = dratio * after * base * base * before * (1.0 - before)
        dafter = -dratio * base * after * (1.0 - after)
        dsigned = (dbefore + dafter) * inv_s
        dhalf = (dafter - dbefore) * inv_s
        vac[0] += dbefore * (signed - half) + dafter * (signed + half)
        vac[1] += dsigned
        dzr[pl.ds(0, RC, stride=16), :] = dsigned
        ddelta = dhalf * slope * 0.5
        dcosine = dhalf * delta * 0.5 * slope_d
        for j in range(NSUB):
            dzb[:, sub(j)] = gather_rows(dzr, 0, j, 16).astype(BF)

        zc[3] = nn(wcl[...], dzb[:, 0:PTS]).astype(BF) * dc[3]
        for l in range(3, 0, -1):
            zc[l - 1] = nn(w[5 + l], zc[l]).astype(BF) * dc[l - 1]
            acc[5 + l] += nt(hc[l - 1], zc[l])
        dd = nn(wcx[...], zc[0]).astype(BF).astype(F32)
        for j in range(NSUB):
            spread_rows(dx, j, EROWS, dd[:, sub(j)])
        accx[...] += nt(fx[...], zc[0])
        accl[0] += nt(dzb[:, 0:PTS], hc[3, 0:H])
        fx[0:H] = nn(w[10], zc[0]).astype(BF)

        dpoint, dview = [], []
        for c in range(3):
            nb = ray_row(dx, 30 + c, EROWS) + dcosine * dcol[c]
            p = ray_row(dx, c, EROWS)
            v = ray_row(dx, 3 + c, EROWS) + dcosine * normal[c]
            eb[pl.ds(c, RC, stride=EROWS), :] = nb
            for k in range(6):
                two = 2.0**k
                sn, cs = feature(3 + 6 * k + c), feature(6 + 6 * k + c)
                eb[pl.ds(3 + 6 * k + c, RC, stride=EROWS), :] = two * cs * nb
                eb[pl.ds(6 + 6 * k + c, RC, stride=EROWS), :] = -two * sn * nb
                p = p - (two * two) * nb * (
                    sn * ray_row(de, 3 + 6 * k + c, EROWS) + cs * ray_row(de, 6 + 6 * k + c, EROWS)
                )
            for k in range(4):
                sn = xt[pl.ds(e0 + 6 + 6 * k + c, RC, stride=EROWS), :]
                cs = xt[pl.ds(e0 + 9 + 6 * k + c, RC, stride=EROWS), :]
                v = v + 2.0**k * (
                    cs * ray_row(dx, 6 + 6 * k + c, EROWS) - sn * ray_row(dx, 9 + 6 * k + c, EROWS)
                )
            dpoint.append(p)
            dview.append(v)

        for j in range(NSUB):
            encb[:, sub2(j)] = gather_rows(eb, 0, j, EROWS).astype(BF)
        for l in range(7):
            if l == 0:
                gg = nn(w0t[...], encb[:, PTS:])
            else:
                gg = nn(wt[l - 1], hx[l - 1, 0:H, PTS:])
            for j in range(NSUB):
                g = gg[:, sub(j)]
                s = ss[l, :, sub(j)]
                if l == 3:
                    g = g * s.astype(F32)
                    x = g.astype(BF)
                else:
                    x = g.astype(BF) * s
                u = wide(w7s[...]).astype(BF) if l == 6 else us[l, :, sub(j)]
                ts[l, :, sub(j)] = x * u * (2.0 - 2.0 * s)
                if l == 3:
                    e = gather_rows(eb, 0, j, EROWS)
                    x = ROOT_HALF * jnp.concatenate([g[0:EROWS] + e, g[EROWS:]], axis=0)
                    x = x.astype(BF)
                hx[l, 0:H, sub2(j)] = x

        dd = nn(w[9], fx[0:H])
        for j in range(NSUB):
            row = gather_rows(dzr, 0, j, 16)[0:1]
            d = dd[:, sub(j)] + wide(w7s[...]) * row
            zg[6, :, sub(j)] = d.astype(BF) * ss[6, :, sub(j)] + ts[6, :, sub(j)]
        acc[9] += nt(hx[6, :, 0:PTS], fx[0:H])
        accl[1] += nt(dzb[...], hx[6, 0:H])
        for l in range(6, 0, -1):
            dd = nn(w[l - 1], zg[l, :, 0:PTS])
            for j in range(NSUB):
                d = dd[:, sub(j)].astype(BF)
                if l == 4:
                    d = d.astype(F32) * ROOT_HALF
                    spread_rows(dx, j, EROWS, d)
                    d = d.astype(BF)
                zg[l - 1, :, sub(j)] = d * ss[l - 1, :, sub(j)] + ts[l - 1, :, sub(j)]
            acc[l - 1] += nt(hx[l - 1], zg[l])
        acc0[...] += nt(encb[...], zg[0])
        dd = nn(w0[...], zg[0, :, 0:PTS]).astype(BF).astype(F32)
        for j in range(NSUB):
            spread_rows(dx, j, EROWS, dd[:, sub(j)] + gather_rows(dx, 0, j, EROWS))

        depth = dep[pl.ds(r0, RC), :]
        ddepth = jnp.zeros((RC, SAMP), F32)
        for c in range(3):
            p = dpoint[c] + ray_row(dx, c, EROWS)
            for k in range(6):
                p = p + 2.0**k * (
                    feature(6 + 6 * k + c) * ray_row(dx, 3 + 6 * k + c, EROWS)
                    - feature(3 + 6 * k + c) * ray_row(dx, 6 + 6 * k + c, EROWS)
                )
            ddepth = ddepth + p * dcol[c]
            v = dview[c] + depth * p
            out = out + jnp.where(lane128 == 3 + c, jnp.sum(p, axis=1, keepdims=True), 0.0)
            out = out + jnp.where(lane128 == 6 + c, jnp.sum(v, axis=1, keepdims=True), 0.0)
        outc[pl.ds(r0, RC), :] = out
        later = exact(ddepth, (iota((SAMP, SAMP), 0) >= iota((SAMP, SAMP), 1)).astype(F32))
        deltag_o[pl.ds(r0, RC), :] = ddelta + later - 0.5 * ddepth
        return carry

    lax.fori_loop(0, rays // RC, chunk, 0)

    result = outc[...].T
    rgb_o[...] = result[0:3, 0:rays]
    ag_o[...] = result[3:6, 0:rays]
    dg_o[...] = result[6:9, 0:rays]
    tail_rows = jnp.where(row8 == 0, accl[1, 0:8], accl[0, 0:8])
    lines = [acc[0, H : H + 1]]
    for k in (0, 1, 4, 5, 3, 0, 6, 7, 8):
        lines.append(acc[k, H : H + 1])
    small_rows = jnp.concatenate(lines, axis=0)
    upper = jnp.concatenate(
        [
            acc0[...],
            jnp.zeros((CROSS - EROWS, H), F32),
            accx[H : H + EROWS],
            jnp.zeros((BIASES - CROSS - EROWS, H), F32),
            small_rows,
            jnp.zeros((TAIL - BIASES - 10, H), F32),
            tail_rows,
            jnp.zeros((H - TAIL - 8, H), F32),
        ],
        axis=0,
    )
    packed = turned(upper.astype(BF))
    groups = [turned(acc[k, 0:H].astype(BF)) for k in (0, 1, 4, 5, 3, 6, 7, 8)]
    groups += [turned(accx[0:H].astype(BF)), packed, acc[2, 0:H], acc[9, 0:H]]

    for q in range(GROUPS // 2):
        pair = [groups[2 * q + t].reshape(H // rp, rp, H) for t in range(2)]
        gout[:, 2 * rp * q : 2 * rp * (q + 1), :] = jnp.concatenate(pair, axis=1).astype(BF)

    def total(k):
        return jnp.sum(jnp.sum(vac[k], axis=1, keepdims=True), axis=0, keepdims=True)

    lane_bias = jnp.zeros((1, H), F32)
    for k in range(4):
        lane_bias = lane_bias + jnp.where(lane256 == TAIL + k, total(1 + k), 0.0)
    variance = jnp.where(lane256 == 0, total(0) * inv_s * 10.0, 0.0)
    tot_o[...] = jnp.concatenate(
        [
            jnp.sum(d3 * acc[2, 0:H], axis=0, keepdims=True),
            acc[2, H : H + 1],
            jnp.sum(d7 * acc[9, 0:H], axis=0, keepdims=True),
            acc[9, H : H + 1],
            jnp.sum(misc * packed, axis=0, keepdims=True),
            lane_bias,
            variance,
            jnp.zeros((1, H), F32),
        ],
        axis=0,
    )


def percol_ref_col(ref, r0, j):
    return jnp.broadcast_to(ref[pl.ds(r0, RC), j : j + 1], (RC, SAMP))


def compute(fsdp, devices, anchors, directions, deltas, foreground, cotangent, smalls, layers):
    rays = deltas.shape[0]
    vm, dma = pltpu.VMEM, pltpu.SemaphoreType.DMA
    rp = layers[0].shape[0]
    points = rays * EROWS
    scratch = [
        vm((devices, GROUPS * rp, H), BF),
        vm((4, rp, 384), F32),
        dma((2, devices)),
        dma((2, devices)),
        vm((GROUPS, H, H), BF),
        vm((8, 384), F32),
        vm((9, H, H), BF),
        vm((11, H, H), BF),
        vm((H + 16, H), BF),
        vm((H, EROWS), BF),
        vm((EROWS, H), BF),
        vm((H, H + EROWS), BF),
        vm((EROWS, H), BF),
        vm((16, H), BF),
        vm((H, 16), BF),
        vm((H, 128), F32),
        vm((10, H, 128), F32),
        vm((points, SAMP), F32),
        vm((ENC, rays, SAMP), F32),
        vm((points, SAMP), F32),
        vm((rays, SAMP), F32),
        vm((128, 128), F32),
        vm((7, H + 16, 2 * PTS), BF),
        vm((7, H, PTS), BF),
        vm((6, H, PTS), BF),
        vm((7, H, 2 * PTS), BF),
        vm((7, H, PTS), BF),
        vm((H + EROWS, PTS), BF),
        vm((4, H + 16, PTS), BF),
        vm((4, H, PTS), BF),
        vm((4, H, PTS), BF),
        vm((EROWS, 2 * PTS), BF),
        vm((16, 2 * PTS), BF),
        vm((RC * EROWS, SAMP), F32),
        vm((RC * EROWS, SAMP), F32),
        vm((RC * 16, SAMP), F32),
        vm((RC * 16, SAMP), F32),
        vm((RC * 16, SAMP), F32),
        vm((RC * EROWS, SAMP), F32),
        vm((RC * EROWS, SAMP), F32),
        vm((128, 128), F32),
        vm((10, H + 16, H), F32),
        vm((EROWS, H), F32),
        vm((H + EROWS, H), F32),
        vm((2, 16, H), F32),
        vm((5, RC, SAMP), F32),
    ]
    shapes = (
        jax.ShapeDtypeStruct((3, rays), F32),
        jax.ShapeDtypeStruct((3, rays), F32),
        jax.ShapeDtypeStruct((3, rays), F32),
        jax.ShapeDtypeStruct((rays, SAMP), F32),
        jax.ShapeDtypeStruct((H // rp, GROUPS * rp, H), BF),
        jax.ShapeDtypeStruct((8, H), F32),
        jax.ShapeDtypeStruct((8, H), F32),
        jax.ShapeDtypeStruct((8, H), F32),
    )
    whole = pl.BlockSpec(memory_space=pltpu.VMEM)
    return pl.pallas_call(
        functools.partial(compute_kernel, fsdp),
        out_shape=shapes,
        in_specs=[whole] * 30,
        out_specs=(whole,) * 8,
        scratch_shapes=scratch,
        name="nets",
        compiler_params=pltpu.CompilerParams(
            collective_id=0, has_side_effects=True, vmem_limit_bytes=62 * 1024 * 1024
        ),
    )(anchors, directions, deltas, foreground, cotangent, *smalls, *layers)


def scatter_kernel(fsdp, g, tot, share, tot_o, rcc, rca, rcb, rcz, tc, ta, tb, tz, send, sc, sa, sb, sz, tsend, trecv):
    place = Place(fsdp)
    z, depth = place.z, place.depth
    barrier = pltpu.get_barrier_semaphore()
    place.greet(barrier)
    place.wait_all(barrier)
    rows = g.shape[1] // 2

    def own(half, k, a, b, c):
        return g.at[place.index(half, place.turn(k), a, b, c), pl.ds(half * rows, rows)]

    def add(x, y):
        return x[...].astype(F32) + y[...].astype(F32)

    def to_core(half, k, a, b):
        slot = k * 4 + a * 2 + b
        return remote(
            own(half, k, a, b, 1), rcc.at[half, slot], send.at[half, slot], sc.at[half, slot],
            place.device(half, z, 0, 0, 1),
        )

    def to_a(half, k, b):
        slot = k * 2 + b
        return remote(
            rcc.at[half, k * 4 + 2 + b], rca.at[half, slot], send.at[half, 4 * depth + slot],
            sa.at[half, slot], place.device(half, z, 1),
        )

    def to_b(half, k):
        return remote(
            rca.at[half, k * 2 + 1], rcb.at[half, k], send.at[half, 6 * depth + k], sb.at[half, k],
            place.device(half, z, 0, 1),
        )

    def to_z(half, k):
        return remote(
            rcb.at[half, k], rcz.at[half, k], send.at[half, 7 * depth + k], sz.at[half, k],
            place.device(half, place.turn(k)),
        )

    def tot_copy(src, dst, k, *to):
        return remote(src, dst, tsend.at[k], trecv.at[k], place.device(0, *to))

    def order(body):
        each(1, depth, body)
        body(0)

    t_core = tot_copy(tot, tc, 0, z, 0, 0, 1)
    t_core.start()
    for a, b in ((1, 1), (1, 0), (0, 1), (0, 0)):

        def start_core(k):
            for half in range(2):
                to_core(half, k, a, b).start()

        order(start_core)

    def join_core(k, a, b):
        for half in range(2):
            slot = k * 4 + a * 2 + b
            to_core(half, k, a, b).wait_recv()
            rcc[half, slot] = add(rcc.at[half, slot], own(half, k, a, b, 0)).astype(BF)
            if a:
                to_a(half, k, b).start()

    order(lambda k: join_core(k, 1, 1))
    order(lambda k: join_core(k, 1, 0))
    t_core.wait()
    tc[...] = tot[...] + tc[...]
    t_a = tot_copy(tc, ta, 1, z, 1)
    t_a.start()
    order(lambda k: join_core(k, 0, 1))
    order(lambda k: join_core(k, 0, 0))
    t_a.wait()
    ta[...] = tc[...] + ta[...]
    t_b = tot_copy(ta, tb, 2, z, 0, 1)
    t_b.start()

    def join_a(k, b):
        for half in range(2):
            slot = k * 2 + b
            to_a(half, k, b).wait_recv()
            rca[half, slot] = add(rca.at[half, slot], rcc.at[half, k * 4 + b]).astype(BF)
            if b:
                to_b(half, k).start()

    order(lambda k: join_a(k, 1))
    t_b.wait()
    tz[z] = ta[...] + tb[...]

    def start_tot(k):
        tot_copy(tz.at[z], tz.at[z], 2 + k, place.turn(k)).start()

    each(1, depth, start_tot)
    order(lambda k: join_a(k, 0))

    def join_b(k):
        for half in range(2):
            to_b(half, k).wait_recv()
            rcb[half, k] = add(rcb.at[half, k], rca.at[half, k * 2]).astype(BF)
            to_z(half, k).start()

    each(1, depth, join_b)
    for half in range(2):
        to_b(half, 0).wait_recv()
        share[half * rows : (half + 1) * rows] = add(rcb.at[half, 0], rca.at[half, 0])

    def join_z(k):
        for half in range(2):
            to_z(half, k).wait_recv()
            share[half * rows : (half + 1) * rows] += rcz[half, k].astype(F32)

    each(1, depth, join_z)

    def end_tot(k):
        tot_copy(tz.at[z], tz.at[z], 2 + k, place.turn(k)).wait()

    each(1, depth, end_tot)
    total = tz[0]
    for k in range(1, depth):
        total = total + tz[k]
    tot_o[...] = total

    def sent(k):
        for half in range(2):
            for a in range(2):
                for b in range(2):
                    to_core(half, k, a, b).wait_send()
            to_a(half, k, 0).wait_send()
            to_a(half, k, 1).wait_send()
            to_b(half, k).wait_send()

    each(0, depth, sent)

    def sent_z(k):
        for half in range(2):
            to_z(half, k).wait_send()

    each(1, depth, sent_z)


def unscaled_rows(d, gain, grad):
    inv = lax.rsqrt(jnp.sum(d * d, axis=1, keepdims=True) + EPS)
    dot = jnp.sum(d * grad, axis=1, keepdims=True)
    return grad * (gain * inv) - d * (gain * inv * inv * inv * dot), dot * inv


def finish_kernel(
    share, tot, inv, smalls, first, mid, narrow, skip, last, cfirst, cmid,
    fg, mg, sg, cg, cmg, cl, rgb, ag, dg, deltag, o_rgb, o_ag, o_dg, o_deltag,
    o_first, o_fg, o_fb, o_mid, o_mg, o_mb, o_narrow, o_ng, o_nb, o_skip, o_sg, o_sb,
    o_last, o_lg, o_lb, o_cfirst, o_cg, o_cb, o_cmid, o_cmg, o_cmb, o_clast, o_clg, o_clb, o_var,
    wid,
):
    r = first.shape[0]
    for src, dst in ((rgb, o_rgb), (ag, o_ag), (dg, o_dg), (deltag, o_deltag)):
        dst[...] = src[...]
    d_first, d_narrow, d_last, d_cfirst = share_rows(first, narrow, last, cfirst, wid)

    def vec(ref, k=None):
        return column(as_row(ref) if k is None else ref[...].astype(F32)[k : k + 1])

    def group(k):
        return share[k * r : (k + 1) * r, :]

    def put(ref, col):
        ref[...] = line(col).reshape(r)

    def put_rows(ref, columns):
        ref[...] = jnp.concatenate([line(col) for col in columns], axis=0)

    misc = group(9)
    lane = iota((1, 128), 1)
    g, gain = unscaled_rows(d_first, vec(fg), jnp.where(lane < ENC, misc[:, 0:128], 0.0))
    o_first[...] = g[:, 0:ENC]
    put(o_fg, gain)
    put(o_fb, misc[:, ENC : ENC + 1])
    gains = []
    for k in range(4):
        g, gain = unscaled_rows(mid[k].astype(F32), vec(mg, k), group(k))
        o_mid[k] = g
        gains.append(gain)
    put_rows(o_mg, gains)
    put_rows(o_mb, [misc[:, BIASES + 1 + k : BIASES + 2 + k] for k in range(4)])
    g, gain = unscaled_rows(skip[...].astype(F32), vec(sg), pltpu.roll(group(4), H - ENC, 1))
    o_skip[...] = g
    put(o_sg, gain)
    put(o_sb, misc[:, BIASES + 5 : BIASES + 6])
    extra = jnp.where(lane < NX, misc[:, 128:256], 0.0)
    moved = jnp.concatenate([group(8), jnp.zeros((r, 128), F32)], axis=1)
    grad = pltpu.roll(moved, NX, 1) + jnp.concatenate([extra, jnp.zeros((r, H), F32)], axis=1)
    g, gain = unscaled_rows(d_cfirst, vec(cg), grad)
    o_cfirst[...] = g[:, 0 : H + NX]
    put(o_cg, gain)
    put(o_cb, misc[:, CROSS + NX : CROSS + NX + 1])
    gains = []
    for k in range(3):
        g, gain = unscaled_rows(cmid[k].astype(F32), vec(cmg, k), group(5 + k))
        o_cmid[k] = g
        gains.append(gain)
    put_rows(o_cmg, gains)
    put_rows(o_cmb, [misc[:, BIASES + 7 + k : BIASES + 8 + k] for k in range(3)])

    def across(k, d, grad):
        gain, iv, dot = smalls[k : k + 1, :], inv[k : k + 1, :], tot[k : k + 1, :]
        return grad * (gain * iv) - d * (gain * iv * iv * iv * dot)

    g = across(0, pltpu.roll(d_narrow, ENC, 1), group(10))
    o_narrow[...] = pltpu.roll(g, H - ENC, 1)[:, 0:NARROW]
    g = across(2, pltpu.roll(d_last, 383, 1)[:, 0:H], group(11))
    right = jnp.where(lane == TAIL - 128, d_last[:, 0:1], 0.0)
    for c in range(3):
        right = right + jnp.where(lane == TAIL - 127 + c, vec(cl, c), 0.0)
    t = across(4, jnp.concatenate([jnp.zeros((r, 128), F32), right], axis=1), misc)
    first_lane = iota((1, 384), 1) == 0

    def behind(x, front):
        more = jnp.zeros((x.shape[0], 128), F32)
        moved = pltpu.roll(jnp.concatenate([x, more], axis=1), 1, 1)
        return jnp.where(first_lane, front, moved)[:, 0 : H + 1]

    o_last[...] = behind(g, t[:, TAIL : TAIL + 1])
    put_rows(o_clast, [t[:, TAIL + 1 + c : TAIL + 2 + c] for c in range(3)])
    gained = tot[...] * inv[...]
    back = pltpu.roll(jnp.concatenate([gained[0:1], tot[1:2], jnp.zeros((6, H), F32)], axis=0), H - ENC, 1)
    o_ng[...] = back[0:1, 0:NARROW].reshape(NARROW)
    o_nb[...] = back[1:2, 0:NARROW].reshape(NARROW)
    eight = jnp.zeros((7, H), F32)
    o_lg[...] = behind(jnp.concatenate([gained[2:3], eight], axis=0), gained[4:5, TAIL : TAIL + 1])[0:1].reshape(H + 1)
    o_lb[...] = behind(jnp.concatenate([tot[3:4], eight], axis=0), tot[5:6, TAIL : TAIL + 1])[0:1].reshape(H + 1)
    tails = jnp.concatenate([gained[4:5], tot[5:6], jnp.zeros((6, H), F32)], axis=0)
    tails = pltpu.roll(tails, H - TAIL - 1, 1)
    o_clg[...] = tails[0:1, 0:3].reshape(3)
    o_clb[...] = tails[1:2, 0:3].reshape(3)
    o_var[...] = tot[6:7, 0:1].reshape(1)


def per_device(
    fsdp, devices,
    anchors, directions, deltas, foreground,
    sdf_first_dir, sdf_first_gain, sdf_first_bias,
    sdf_mid_dir, sdf_mid_gain, sdf_mid_bias,
    sdf_narrow_dir, sdf_narrow_gain, sdf_narrow_bias,
    sdf_skip_dir, sdf_skip_gain, sdf_skip_bias,
    sdf_last_dir, sdf_last_gain, sdf_last_bias,
    color_first_dir, color_first_gain, color_first_bias,
    color_mid_dir, color_mid_gain, color_mid_bias,
    color_last_dir, color_last_gain, color_last_bias,
    variance, rgb_cotangent,
):
    r = sdf_first_gain.shape[0]
    rp = max(r, 8)
    depth = fsdp // 2
    whole = pl.BlockSpec(memory_space=pltpu.VMEM)
    vm, dma = pltpu.VMEM, pltpu.SemaphoreType.DMA

    def rows(x):
        return x if rp == r else jnp.pad(x, [(0, 0)] * (x.ndim - 2) + [(0, rp - r), (0, 0)])

    def lanes(x):
        return x if rp == r else jnp.pad(x, [(0, 0)] * (x.ndim - 1) + [(0, rp - r)])

    shares = (
        rows(sdf_first_dir.T),
        rows(jnp.swapaxes(sdf_mid_dir, 1, 2)),
        rows(sdf_narrow_dir),
        rows(sdf_skip_dir.T),
        rows(sdf_last_dir),
        rows(color_first_dir.T),
        rows(jnp.swapaxes(color_mid_dir, 1, 2)),
    )
    fg, fb, mg, mb, sg, sb, cg, cb, cmg, cmb, cl = (
        lanes(x)
        for x in (
            sdf_first_gain, sdf_first_bias, sdf_mid_gain, sdf_mid_bias, sdf_skip_gain, sdf_skip_bias,
            color_first_gain, color_first_bias, color_mid_gain, color_mid_bias, color_last_dir.T,
        )
    )
    size = GROUPS * rp
    limit = 60 * 1024 * 1024
    blocks = H // rp

    def ungroup(x):
        if rp == r:
            return x
        x = x.reshape(blocks, GROUPS, devices // blocks, r, H).transpose(0, 2, 1, 3, 4)
        return rows(x).reshape(devices, size, H)

    rgb, ag, dg, deltag, gout, tot, inv, smalls = compute(
        fsdp, devices, anchors, directions, deltas, foreground, rgb_cotangent,
        (
            variance, sdf_narrow_gain, sdf_narrow_bias, sdf_last_gain, sdf_last_bias,
            color_last_gain, color_last_bias,
        ),
        (*shares, fg, fb, mg, mb, sg, sb, cg, cb, cmg, cmb, cl),
    )
    half = size // 2
    share, tot = pl.pallas_call(
        functools.partial(scatter_kernel, fsdp),
        out_shape=(jax.ShapeDtypeStruct((size, H), F32), jax.ShapeDtypeStruct((8, H), F32)),
        in_specs=[whole] * 2,
        out_specs=(whole,) * 2,
        scratch_shapes=[
            vm((2, 4 * depth, half, H), BF),
            vm((2, 2 * depth, half, H), BF),
            vm((2, depth, half, H), BF),
            vm((2, depth, half, H), BF),
            vm((8, H), F32),
            vm((8, H), F32),
            vm((8, H), F32),
            vm((depth, 8, H), F32),
            dma((2, 8 * depth)),
            dma((2, 4 * depth)),
            dma((2, 2 * depth)),
            dma((2, depth)),
            dma((2, depth)),
            dma((2 + depth,)),
            dma((2 + depth,)),
        ],
        name="scatter",
        compiler_params=pltpu.CompilerParams(
            collective_id=1, has_side_effects=True, vmem_limit_bytes=limit
        ),
    )(ungroup(gout), tot)

    def f32(*shape):
        return jax.ShapeDtypeStruct(shape, F32)

    outs = pl.pallas_call(
        finish_kernel,
        out_shape=(
            f32(*rgb.shape), f32(*ag.shape), f32(*dg.shape), f32(*deltag.shape),
            f32(rp, ENC), f32(rp), f32(rp),
            f32(4, rp, H), f32(4, rp), f32(4, rp),
            f32(rp, NARROW), f32(NARROW), f32(NARROW),
            f32(rp, H), f32(rp), f32(rp),
            f32(rp, H + 1), f32(H + 1), f32(H + 1),
            f32(rp, H + NX), f32(rp), f32(rp),
            f32(3, rp, H), f32(3, rp), f32(3, rp),
            f32(3, rp), f32(3), f32(3),
            f32(1),
        ),
        in_specs=[whole] * 21,
        out_specs=(whole,) * 29,
        scratch_shapes=[vm((4, rp, 384), F32)],
        name="finish",
    )(share, tot, inv, smalls, *shares, fg, mg, sg, cg, cmg, cl, rgb, ag, dg, deltag)
    (
        rgb, ag, dg, deltag,
        o_first, o_fg, o_fb, o_mid, o_mg, o_mb, o_narrow, o_ng, o_nb, o_skip, o_sg, o_sb,
        o_last, o_lg, o_lb, o_cfirst, o_cg, o_cb, o_cmid, o_cmg, o_cmb, o_clast, o_clg, o_clb, o_var,
    ) = outs
    return (
        rgb, ag, dg, deltag,
        o_first[0:r].T, o_fg[0:r], o_fb[0:r],
        jnp.swapaxes(o_mid[:, 0:r], 1, 2), o_mg[:, 0:r], o_mb[:, 0:r],
        o_narrow[0:r], o_ng, o_nb,
        o_skip[0:r].T, o_sg[0:r], o_sb[0:r],
        o_last[0:r], o_lg, o_lb,
        o_cfirst[0:r].T, o_cg[0:r], o_cb[0:r],
        jnp.swapaxes(o_cmid[:, 0:r], 1, 2), o_cmg[:, 0:r], o_cmb[:, 0:r],
        o_clast[:, 0:r].T, o_clg, o_clb,
        o_var,
    )


def solution(mesh):
    fsdp, rep = mesh.shape["fsdp"], mesh.shape["rep"]
    assert rep == 4 and fsdp % 2 == 0
    both = ("fsdp", "rep")
    cols, vec, cols3, rows, copied = P(None, both), P(both), P(None, None, both), P(both, None), P()
    layers = (
        cols, vec, vec, cols3, cols, cols, rows, copied, copied, cols, vec, vec,
        rows, copied, copied, cols, vec, vec, cols3, cols, cols, rows, copied, copied,
    )
    return jax.shard_map(
        functools.partial(per_device, fsdp, fsdp * rep),
        mesh=mesh,
        in_specs=(cols, cols, rows, rows) + layers + (copied, cols),
        out_specs=(cols, cols, cols, rows) + layers + (copied,),
        check_vma=False,
    )
```

```python
import functools

import jax
import jax.numpy as jnp
from jax import lax
from jax.experimental import pallas as pl
from jax.experimental.pallas import tpu as pltpu
from jax.sharding import PartitionSpec as P

F32 = jnp.float32
BF = jnp.bfloat16
H = 256
SAMP = 128
ENC = 39
EROWS = 48
NARROW = 217
NX = 33
GROUPS = 12
SUB = 256
PAIRS = ((6, 7), (5, 8), (11, 3), (2, 4), (10, 1), (0, 9))
RSUB = SUB // SAMP
CROSS = 128
BIASES = 200
TAIL = 216
EPS = 1e-06
HALF_LN2 = 0.34657359027997264
ROOT_HALF = 0.7071067811865476


def nn(a, b):
    return lax.dot_general(a, b, (((1,), (0,)), ((), ())), preferred_element_type=F32)


def nt(a, b):
    return lax.dot_general(a, b, (((1,), (1,)), ((), ())), preferred_element_type=F32)


def exact(a, b):
    return lax.dot_general(
        a, b, (((1,), (0,)), ((), ())), precision=lax.Precision.HIGHEST, preferred_element_type=F32
    )


def iota(shape, dim):
    return lax.broadcasted_iota(jnp.int32, shape, dim)


def column(row):
    n = row.shape[1]
    return jnp.sum(jnp.where(iota((n, n), 0) == iota((n, n), 1), row, 0.0), axis=1, keepdims=True)


def as_row(ref):
    return ref[...].astype(F32).reshape(1, ref.shape[0])


def line(col):
    n = col.shape[0]
    return jnp.sum(jnp.where(iota((n, n), 0) == iota((n, n), 1), col, 0.0), axis=0, keepdims=True)


def wide(half):
    return jnp.concatenate([half, half], axis=1)


def sharp(z):
    z = z.astype(BF)
    s = 0.5 * jnp.tanh(z) + 0.5
    return jnp.maximum(z, 0.0) - 0.5 * jnp.log(jnp.maximum(s, 1.0 - s)), s


def silu(z):
    z = z.astype(BF)
    g = 0.5 * jnp.tanh(0.5 * z) + 0.5
    h = z * g
    return h, g + h * (1.0 - g)


def softplus(x):
    return jnp.maximum(x, 0.0) + jnp.log(1.0 + jnp.exp(-jnp.abs(x)))


def sigmoid(x):
    return 1.0 / (1.0 + jnp.exp(-x))


def scaled_rows(d, gain):
    return d * (gain * lax.rsqrt(jnp.sum(d * d, axis=1, keepdims=True) + EPS))


def share_rows(first, narrow, last, cfirst, wid):
    r = first.shape[0]

    def padded(k, ref, lanes):
        wid[k] = jnp.zeros(wid.shape[1:], F32)
        wid[k, :, 0 : ref.shape[1]] = ref[...].astype(F32)
        return wid[k][:, 0:lanes]

    return (padded(0, first, 128), padded(1, narrow, H), padded(2, last, 384), padded(3, cfirst, 384))


class Place:
    def __init__(self, fsdp):
        f, p = lax.axis_index("fsdp"), lax.axis_index("rep")
        self.depth = fsdp // 2
        self.z, self.y, self.x, self.c = f // 2, f % 2, p // 2, p % 2

    def at(self, half, z, a=0, b=0, c=0):
        dy, dx = (a, b) if half == 0 else (b, a)
        return z, (self.y + dy) % 2, (self.x + dx) % 2, (self.c + c) % 2

    def index(self, *where):
        z, y, x, c = self.at(*where)
        return ((z * 2 + y) * 2 + x) * 2 + c

    def device(self, *where):
        z, y, x, c = self.at(*where)
        return z * 2 + y, x * 2 + c

    def turn(self, k):
        return (self.z + k) % self.depth

    def greet(self, barrier):
        def one(k, carry):
            signal(barrier, self.device(0, self.turn(k)))
            return carry

        lax.fori_loop(1, self.depth, one, 0)
        for flips in ((1, 0, 0), (0, 1, 0), (0, 0, 1)):
            signal(barrier, self.device(0, self.z, *flips))

    def wait_all(self, barrier):
        pl.semaphore_wait(barrier, self.depth + 2)


def signal(sem, device):
    pl.semaphore_signal(sem, inc=1, device_id=device, device_id_type=pl.DeviceIdType.MESH)


def remote(src, dst, send, recv, device):
    return pltpu.make_async_remote_copy(
        src_ref=src, dst_ref=dst, send_sem=send, recv_sem=recv,
        device_id=device, device_id_type=pl.DeviceIdType.MESH,
    )


def each(start, stop, body):
    def one(k, carry):
        body(k)
        return carry

    lax.fori_loop(start, stop, one, 0)


def own_share(
    first, mid, narrow, skip, last, cfirst, cmid, fg, fb, mg, mb, sg, sb, cg, cb, cmg, cmb, cl, wid
):
    d_first, d_narrow, d_last, d_cfirst = share_rows(first, narrow, last, cfirst, wid)

    def vec(ref, k=None):
        row = as_row(ref) if k is None else ref[...].astype(F32)[k : k + 1]
        return column(row)

    lane = iota((1, 128), 1)
    parts = [scaled_rows(mid[k].astype(F32), vec(mg, k)) for k in range(4)]
    parts.append(pltpu.roll(scaled_rows(skip[...].astype(F32), vec(sg)), ENC, 1))
    parts += [scaled_rows(cmid[k].astype(F32), vec(cmg, k)) for k in range(3)]
    s_cfirst = scaled_rows(d_cfirst, vec(cg))
    parts.append(pltpu.roll(s_cfirst, 384 - NX, 1)[:, 0:H])
    left = scaled_rows(d_first, vec(fg)) + jnp.where(lane == ENC, vec(fb), 0.0)
    right = jnp.where(lane < NX, s_cfirst[:, 0:128], 0.0) + jnp.where(lane == NX, vec(cb), 0.0)
    biases = [(1, mb, 0), (2, mb, 1), (3, mb, 2), (4, mb, 3), (5, sb, None), (7, cmb, 0), (8, cmb, 1), (9, cmb, 2)]
    for j, ref, k in biases:
        right = right + jnp.where(lane == BIASES - 128 + j, vec(ref, k), 0.0)
    right = right + jnp.where(lane == TAIL - 128, d_last[:, 0:1], 0.0)
    for c in range(3):
        right = right + jnp.where(lane == TAIL - 127 + c, vec(cl, c), 0.0)
    parts.append(jnp.concatenate([left, right], axis=1))
    parts.append(pltpu.roll(d_narrow, ENC, 1))
    parts.append(pltpu.roll(d_last, 383, 1)[:, 0:H])
    return [jnp.concatenate([parts[k] for k in pair], axis=0).astype(BF) for pair in PAIRS]


def gather(place, out, send, recv, meanwhile):
    z, depth = place.z, place.depth
    me = place.index(0, z)
    def copy(half, slab, s, *to):
        part = out.at[pl.ds(half * 3, 3), slab]
        return remote(part, part, send.at[half, s], recv.at[half, slab], place.device(half, *to))

    def arrived(half, slab):
        copy(half, slab, 0, z, 0, 0, 1).wait_recv()

    def along_z(k):
        for half in range(2):
            copy(half, me, k - 1, place.turn(k)).start()

    def pass_on(half, slab, t, stage):
        base = depth - 1
        if stage == 0:
            copy(half, slab, base + t, z, 1).start()
        if stage <= 1:
            copy(half, slab, base + depth + 2 * t + stage, z, 0, 1).start()
        copy(half, slab, base + 3 * depth + 4 * t + stage, z, 0, 0, 1).start()

    each(1, depth, along_z)
    for half in range(2):
        pass_on(half, me, 0, 0)

    def from_z(k):
        for half in range(2):
            slab = place.index(half, place.turn(k))
            arrived(half, slab)
            pass_on(half, slab, k, 0)

    def from_a(k):
        for half in range(2):
            slab = place.index(half, place.turn(k), 1)
            arrived(half, slab)
            pass_on(half, slab, k, 1)

    def from_b(k):
        for half in range(2):
            slab = place.index(half, place.turn(k), 0, 1)
            arrived(half, slab)
            pass_on(half, slab, k, 2)

    def from_ab(k):
        for half in range(2):
            slab = place.index(half, place.turn(k), 1, 1)
            arrived(half, slab)
            pass_on(half, slab, k, 3)

    def from_core(k):
        for half in range(2):
            for a in range(2):
                for b in range(2):
                    arrived(half, place.index(half, place.turn(k), a, b, 1))

    def sent(s):
        for half in range(2):
            copy(half, me, s, z, 0, 0, 1).wait_send()

    meanwhile()
    each(1, depth, from_z)
    each(0, depth, from_a)
    each(0, depth, from_b)
    each(0, depth, from_ab)
    each(0, depth, from_core)
    each(0, 8 * depth - 1, sent)


class Reduction:
    def __init__(self, place, g, share, rcc, rca, rcb, rcz, send, sc, sa, sb, sz):
        self.place, self.g, self.share = place, g, share
        self.rcc, self.rca, self.rcb, self.rcz = rcc, rca, rcb, rcz
        self.send, self.sc, self.sa, self.sb, self.sz = send, sc, sa, sb, sz

    def side(self, q):
        place = self.place
        return (place.y, place.x) if q % 2 == 0 else (place.x, place.y)

    def to_core(self, q, t):
        n, place = 2 * self.place.depth, self.place
        at = ((place.c + 1) % 2) * 2 + (self.side(q)[0] + t) % 2
        return remote(
            self.g.at[q, pl.ds(at * n, n)], self.rcc.at[q, t], self.send.at[q, t], self.sc.at[q, t],
            place.device(q % 2, place.z, 0, 0, 1),
        )

    def to_a(self, q):
        return remote(
            self.rcc.at[q, 1], self.rca.at[q], self.send.at[q, 2], self.sa.at[q],
            self.place.device(q % 2, self.place.z, 1),
        )

    def to_b(self, q):
        n = self.place.depth
        at = (self.side(q)[1] + 1) % 2
        return remote(
            self.rca.at[q, pl.ds(at * n, n)], self.rcb.at[q], self.send.at[q, 3], self.sb.at[q],
            self.place.device(q % 2, self.place.z, 0, 1),
        )

    def to_z(self, q, k):
        to = self.place.turn(k)
        return remote(
            self.rcb.at[q, to], self.rcz.at[q, k], self.send.at[q, 3 + k], self.sz.at[q, k],
            self.place.device(0, to),
        )

    def begin(self, q, first, second):
        depth = self.place.depth
        count = depth * 8
        r, rp = H // count, self.g.shape[2] // 2
        for d in range(count):
            z, y, x, c = d // 8, d // 4 % 2, d // 2 % 2, d % 2
            a, b = (y, x) if q % 2 == 0 else (x, y)
            parts = []
            for m in (first, second):
                parts.append(m[d * r : (d + 1) * r])
                if rp > r:
                    parts.append(jnp.zeros((rp - r, H), F32))
            self.g[q, ((c * 2 + a) * 2 + b) * depth + z] = jnp.concatenate(parts, axis=0).astype(BF)
        self.to_core(q, 1).start()
        self.to_core(q, 0).start()

    def own(self, q, t):
        n = 2 * self.place.depth
        return self.g[q, pl.ds((self.place.c * 2 + (self.side(q)[0] + t) % 2) * n, n)].astype(F32)

    def step_a(self, q):
        self.to_core(q, 1).wait_recv()
        self.rcc[q, 1] = (self.rcc[q, 1].astype(F32) + self.own(q, 1)).astype(BF)
        self.to_a(q).start()
        self.to_core(q, 0).wait_recv()
        self.rcc[q, 0] = (self.rcc[q, 0].astype(F32) + self.own(q, 0)).astype(BF)

    def add_a(self, q, t):
        n = self.place.depth
        at = pl.ds(((self.side(q)[1] + t) % 2) * n, n)
        self.rca[q, at] = (self.rca[q, at].astype(F32) + self.rcc[q, 0, at].astype(F32)).astype(BF)

    def step_b(self, q):
        self.to_a(q).wait_recv()
        self.add_a(q, 1)
        self.to_b(q).start()
        self.add_a(q, 0)

    def step_z(self, q):
        n, z = self.place.depth, self.place.z
        self.to_b(q).wait_recv()
        at = pl.ds(self.side(q)[1] * n, n)
        self.rcb[q] = (self.rcb[q].astype(F32) + self.rca[q, at].astype(F32)).astype(BF)
        each(1, n, lambda k: self.to_z(q, k).start())
        rows = self.g.shape[2]
        self.share[q * rows : (q + 1) * rows] = self.rcb[q, z].astype(F32)

    def step_end(self, q):
        rows = self.g.shape[2]

        def one(k):
            self.to_z(q, k).wait_recv()
            self.share[q * rows : (q + 1) * rows] += self.rcz[q, k].astype(F32)

        each(1, self.place.depth, one)

    def settle(self, q):
        for t in range(2):
            self.to_core(q, t).wait_send()
        self.to_a(q).wait_send()
        self.to_b(q).wait_send()
        each(1, self.place.depth, lambda k: self.to_z(q, k).wait_send())


class Total:
    def __init__(self, place, tc, ta, tb, tz, own, send, recv):
        self.place, self.bufs, self.own = place, (tc, ta, tb), own
        self.tz, self.send, self.recv = tz, send, recv

    def step(self, k):
        to = ((0, 0, 1), (1, 0, 0), (0, 1, 0))[k]
        return remote(
            self.own.at[k], self.bufs[k], self.send.at[k], self.recv.at[k],
            self.place.device(0, self.place.z, *to),
        )

    def begin(self, value):
        self.own[0] = value
        self.step(0).start()

    def go_on(self, k):
        self.step(k).wait()
        value = self.own[k] + self.bufs[k][...]
        if k < 2:
            self.own[k + 1] = value
            self.step(k + 1).start()
        else:
            self.tz[self.place.z] = value
            each(1, self.place.depth, lambda k: self.along(k).start())

    def along(self, k):
        mine = self.tz.at[self.place.z]
        return remote(
            mine, mine, self.send.at[2 + k], self.recv.at[2 + k], self.place.device(0, self.place.turn(k))
        )

    def end(self):
        each(1, self.place.depth, lambda k: self.along(k).wait())
        total = self.tz[0]
        for k in range(1, self.place.depth):
            total = total + self.tz[k]
        return total


def compute_kernel(
    fsdp, rc, anch, dirs, delt, fore, cot, var, ng, nb, lg, lb, cg, cb, *rest
):
    layers, rest = rest[:18], rest[18:]
    compute_body(fsdp, rc, layers, anch, dirs, delt, fore, cot, var, ng, nb, lg, lb, cg, cb, *rest)


def compute_body(
    fsdp, RC, layers, anch, dirs, delt, fore, cot, var, ng, nb, lg, lb, cg, cb,
    rgb_o, ag_o, dg_o, deltag_o, share_o, tot_o, inv_o, smalls,
    gathered, wid, send, recv,
    rcc, rca, rcb, rcz, rsend, sc, sa, sb, sz, tc, ta, tb, tz, town, tsend, trecv, wts, sm, wt, w, wt7, w0t, w0, wcft, wcx, wclt, wcl, w7s, bb,
    enc, fe, xt, dep, cols,
    hx, ss, us, zg, ts, fx, hc, dc, zc, encb, dzb,
    de, nr, row7, rowc, dzr, dx, eb, outc,
    acc, acc0, accx, accl, vac,
):
    rays = delt.shape[0]
    PTS = RC * SAMP
    NSUB = PTS // SUB
    lane128 = iota((1, 128), 1)

    place = Place(fsdp)
    barrier = pltpu.get_barrier_semaphore()
    place.greet(barrier)
    for q, part in enumerate(own_share(*layers, wid)):
        gathered[q, place.index(0, place.z)] = part
    place.wait_all(barrier)

    def meanwhile():
        cols[...] = jnp.zeros(cols.shape, F32)
        cols[0:3, 0:rays] = anch[...]
        cols[3:6, 0:rays] = dirs[...]
        cols[6:9, 0:rays] = cot[...]
        percol = cols[...].T
        cols[...] = percol
        low = (iota((SAMP, SAMP), 0) <= iota((SAMP, SAMP), 1)).astype(F32)
        dall = delt[...]
        depth = 0.1 + exact(dall, low) - 0.5 * dall
        dep[...] = depth
        enc[...] = jnp.zeros(enc.shape, F32)
        xt[...] = jnp.zeros(xt.shape, F32)
        enc[pl.ds(ENC, rays, stride=EROWS), :] = jnp.ones((rays, SAMP), F32)
        xt[pl.ds(NX, rays, stride=EROWS), :] = jnp.ones((rays, SAMP), F32)

        def put_enc(f, value):
            fe[f] = value
            enc[pl.ds(f, rays, stride=EROWS), :] = value

        for c in range(3):
            view = jnp.broadcast_to(percol[0:rays, 3 + c : 4 + c], (rays, SAMP))
            p = percol[0:rays, c : c + 1] + depth * view
            put_enc(c, p)
            xt[pl.ds(c, rays, stride=EROWS), :] = p
            sn, cs = jnp.sin(p), jnp.cos(p)
            for k in range(6):
                put_enc(3 + 6 * k + c, sn)
                put_enc(6 + 6 * k + c, cs)
                sn, cs = 2.0 * sn * cs, 1.0 - 2.0 * sn * sn
            xt[pl.ds(3 + c, rays, stride=EROWS), :] = view
            sn, cs = jnp.sin(view), jnp.cos(view)
            for k in range(4):
                xt[pl.ds(6 + 6 * k + c, rays, stride=EROWS), :] = sn
                xt[pl.ds(9 + 6 * k + c, rays, stride=EROWS), :] = cs
                sn, cs = 2.0 * sn * cs, 1.0 - 2.0 * sn * sn

        nr[...] = jnp.zeros(nr.shape, F32)
        eb[...] = jnp.zeros(eb.shape, F32)
        dzr[...] = jnp.zeros(dzr.shape, F32)
        acc[...] = jnp.zeros(acc.shape, F32)
        acc0[...] = jnp.zeros(acc0.shape, F32)
        accx[...] = jnp.zeros(accx.shape, F32)
        accl[...] = jnp.zeros(accl.shape, F32)
        vac[...] = jnp.zeros(vac.shape, F32)
        hx[:, H : H + 16, 0:PTS] = jnp.ones((7, 16, PTS), BF)
        hx[:, H : H + 16, PTS:] = jnp.zeros((7, 16, PTS), BF)
        dzb[:, PTS:] = jnp.where(iota((16, PTS), 0) == 0, 1.0, 0.0).astype(BF)
        hc[:, H : H + 16, :] = jnp.ones((4, 16, PTS), BF)

    gather(place, gathered, send, recv, meanwhile)

    lane256 = iota((1, H), 1)
    sm[...] = jnp.zeros(sm.shape, F32)
    for k, ref in enumerate((ng, nb, lg, lb, cg, cb)):
        sm[k : k + 1, 0 : ref.shape[0]] = as_row(ref)
    near = pltpu.roll(sm[:, 0:H], H - NARROW, 1)
    tail_row = []
    for k in (0, 1):
        t = jnp.where(lane256 == TAIL, sm[2 + k : 3 + k, 0:1], 0.0)
        for c in range(3):
            t = t + jnp.where(lane256 == TAIL + 1 + c, sm[4 + k : 5 + k, c : c + 1], 0.0)
        tail_row.append(t)
    smalls[...] = jnp.concatenate(
        [
            near[0:1],
            near[1:2] + jnp.where(lane256 < ENC, -1e4, 0.0),
            pltpu.roll(sm[...], 383, 1)[2:4, 0:H],
            tail_row[0],
            tail_row[1],
            jnp.broadcast_to(as_row(var), (1, H)),
            jnp.zeros((1, H), F32),
        ],
        axis=0,
    )
    r = H // gathered.shape[1]
    rp = gathered.shape[2] // 2
    for q, groups in enumerate(PAIRS):
        pair = gathered[q].astype(F32)
        wts[groups[0]] = pair[:, 0:r].reshape(H, H).astype(BF)
        wts[groups[1]] = pair[:, rp : rp + r].reshape(H, H).astype(BF)

    unit = (iota((H, H), 0) == iota((H, H), 1)).astype(BF)

    def turned(x):
        return nt(unit, x)

    misc = wts[9].astype(F32)
    misct = turned(wts[9])
    for k, src in enumerate((0, 1, None, 4, 2, 3, 5, 6, 7)):
        if src is not None:
            wt[k] = wts[src]
            w[k] = turned(wts[src]).astype(BF)
    d3 = wts[10].astype(F32)
    inv3 = lax.rsqrt(jnp.sum(d3 * d3, axis=0, keepdims=True) + EPS)
    w3 = (d3 * (smalls[0:1, :] * inv3)).astype(BF)
    w[2] = w3
    wt[2] = turned(w3).astype(BF)
    d7 = wts[11].astype(F32)
    inv7 = lax.rsqrt(jnp.sum(d7 * d7, axis=0, keepdims=True) + EPS)
    w7 = (d7 * (smalls[2:3, :] * inv7)).astype(BF)
    w[9] = w7
    wt7[0:H] = turned(w7).astype(BF)
    w[10] = turned(wts[8]).astype(BF)
    invm = lax.rsqrt(jnp.sum(misc * misc, axis=0, keepdims=True) + EPS)
    tail = (misc * (smalls[4:5, :] * invm)).astype(BF)
    tailt = turned(tail)[TAIL : TAIL + 8]
    tail = tail.astype(F32)
    row8 = iota((8, H), 0)
    none8 = jnp.zeros((8, H), F32)
    wt7[H : H + 16] = jnp.concatenate([jnp.where(row8 == 0, tailt, 0.0), none8], axis=0).astype(BF)
    wclt[...] = jnp.concatenate(
        [jnp.where((row8 > 0) & (row8 < 4), tailt, 0.0), none8], axis=0
    ).astype(BF)
    only = jnp.where((lane256 > TAIL) & (lane256 < TAIL + 4), tail, 0.0)
    wcl[...] = pltpu.roll(only, H - TAIL, 1)[:, 0:16].astype(BF)
    w7s[...] = jnp.broadcast_to(tail[:, TAIL : TAIL + 1], (H, 128))
    w0t[...] = misc[:, 0:EROWS].astype(BF)
    w0[...] = misct[0:EROWS].astype(BF)
    wcx[...] = misct[CROSS : CROSS + EROWS].astype(BF)
    wcft[:, 0:H] = wts[8]
    wcft[:, H : H + EROWS] = misc[:, CROSS : CROSS + EROWS].astype(BF)
    for k, j in enumerate((1, 2, None, 5, 3, 4, None, 7, 8, 9)):
        if j is not None:
            bb[k] = jnp.broadcast_to(misc[:, BIASES + j : BIASES + j + 1], (H, 128))
    bb[2] = jnp.broadcast_to(column(smalls[1:2, :]), (H, 128))
    bb[6] = jnp.broadcast_to(column(smalls[3:4, :]), (H, 128))
    inv_o[...] = jnp.concatenate([inv3, inv3, inv7, inv7, invm, invm, invm, invm], axis=0)

    inv_s = jnp.exp(10.0 * smalls[6:7, 0:1])

    reduction = Reduction(place, gathered, share_o, rcc, rca, rcb, rcz, rsend, sc, sa, sb, sz)

    def grad_of(k):
        return turned(acc[k, 0:H].astype(BF))

    def chunk(i, last):
        if last:
            r0, e0 = i * RC, i * RC * EROWS
        else:
            r0 = pl.multiple_of(i * RC, RC)
            e0 = pl.multiple_of(i * (RC * EROWS), 8)

        def sub(j):
            return slice(j * SUB, (j + 1) * SUB)

        def sub2(j):
            return slice(PTS + j * SUB, PTS + (j + 1) * SUB)

        def gather_rows(ref, base, j, count):
            start = base + j * RSUB * count
            if not isinstance(start, int):
                start = pl.multiple_of(start, 8)
                return jnp.concatenate(
                    [ref[pl.ds(pl.multiple_of(start + t * count, 8), count), :] for t in range(RSUB)],
                    axis=1,
                )
            return jnp.concatenate(
                [ref[start + t * count : start + (t + 1) * count, :] for t in range(RSUB)], axis=1
            )

        def spread_rows(ref, j, count, value):
            for t in range(RSUB):
                at = (j * RSUB + t) * count
                ref[at : at + count, :] = value[0:count, t * SAMP : (t + 1) * SAMP]

        def ray_row(ref, f, count):
            return ref[pl.ds(f, RC, stride=count), :]

        for j in range(NSUB):
            encb[:, sub(j)] = gather_rows(enc, e0, j, EROWS).astype(BF)
        for l in range(7):
            if l == 0:
                zz = nn(w0t[...], encb[:, 0:PTS])
            else:
                zz = nn(wt[l - 1], hx[l - 1, 0:H, 0:PTS])
            for j in range(NSUB):
                z = zz[:, sub(j)]
                if l > 0:
                    z = z + wide(bb[l - 1])
                h, s = sharp(z)
                ss[l, :, sub(j)] = s.astype(BF)
                if l == 3:
                    e = gather_rows(enc, e0, j, EROWS)
                    keep = iota((EROWS, 1), 0) < ENC
                    h = h.astype(F32)
                    h = ROOT_HALF * jnp.concatenate(
                        [h[0:EROWS] + jnp.where(keep, e, 0.0), h[EROWS:]], axis=0
                    )
                hx[l, 0:H, sub(j)] = h.astype(BF)
        zz = nn(wt7[...], hx[6, 0:H, 0:PTS])
        for j in range(NSUB):
            z = zz[:, sub(j)]
            fx[0:H, sub(j)] = (z[0:H] + wide(bb[6])).astype(BF)
            spread_rows(row7, j, 16, z[H : H + 16])

        for j in range(NSUB):
            zg[6, :, sub2(j)] = wide(w7s[...]).astype(BF) * ss[6, :, sub(j)]
        for l in range(6, 0, -1):
            uu = nn(w[l - 1], zg[l, :, PTS:])
            for j in range(NSUB):
                u = uu[:, sub(j)].astype(BF)
                if l == 4:
                    u = u.astype(F32) * ROOT_HALF
                    spread_rows(de, j, EROWS, u)
                    u = u.astype(BF)
                us[l - 1, :, sub(j)] = u
                zg[l - 1, :, sub2(j)] = u * ss[l - 1, :, sub(j)]
        dd = nn(w0[...], zg[0, :, PTS:]).astype(BF).astype(F32)
        for j in range(NSUB):
            d = dd[:, sub(j)]
            spread_rows(de, j, EROWS, d + gather_rows(de, 0, j, EROWS))

        def feature(f):
            return fe[f, pl.ds(r0, RC), :]

        def ray_col(j):
            return jnp.broadcast_to(cols[pl.ds(r0, RC), j : j + 1], (RC, SAMP))

        dcol = [ray_col(3 + c) for c in range(3)]
        ccol = [ray_col(6 + c) for c in range(3)]
        normal = []
        for c in range(3):
            n = ray_row(de, c, EROWS)
            for k in range(6):
                n = n + 2.0**k * (
                    feature(6 + 6 * k + c) * ray_row(de, 3 + 6 * k + c, EROWS)
                    - feature(3 + 6 * k + c) * ray_row(de, 6 + 6 * k + c, EROWS)
                )
            normal.append(n)
            nr[pl.ds(30 + c, RC, stride=EROWS), :] = n

        delta = delt[pl.ds(r0, RC), :]
        front = fore[pl.ds(r0, RC), :].astype(F32)
        signed = ray_row(row7, 0, 16) + smalls[5:6, TAIL : TAIL + 1]
        cosine = dcol[0] * normal[0] + dcol[1] * normal[1] + dcol[2] * normal[2]
        slope = softplus(-10.0 * cosine) * -0.1
        slope_d = sigmoid(-10.0 * cosine)
        half = slope * delta * 0.5
        before = sigmoid((signed - half) * inv_s)
        after = sigmoid((signed + half) * inv_s)
        ratio = (before - after + 1e-05) / (before + 1e-05)
        ratio_d = front * (sigmoid(20.0 * ratio) - sigmoid(20.0 * (ratio - 1.0)))
        opacity = front * (softplus(20.0 * ratio) - softplus(20.0 * (ratio - 1.0))) * 0.05
        factor = 1.0 - opacity + 1e-07
        survive = factor
        lane = iota((RC, SAMP), 1)
        step = 1
        while step < SAMP:
            survive = survive * jnp.where(lane >= step, pltpu.roll(survive, step, 1), 1.0)
            step *= 2
        through = jnp.where(lane >= 1, pltpu.roll(survive, 1, 1), 1.0)
        contrib = opacity * through

        for j in range(NSUB):
            x = gather_rows(xt, e0, j, EROWS) + gather_rows(nr, 0, j, EROWS)
            fx[H : H + EROWS, sub(j)] = x.astype(BF)
        for l in range(4):
            if l == 0:
                zz = nn(wcft[...], fx[...])
            else:
                zz = nn(wt[5 + l], hc[l - 1, 0:H])
            for j in range(NSUB):
                z = zz[:, sub(j)]
                if l > 0:
                    z = z + wide(bb[6 + l])
                h, d = silu(z)
                hc[l, 0:H, sub(j)] = h.astype(BF)
                dc[l, :, sub(j)] = d.astype(BF)
        zz = nn(wclt[...], hc[3, 0:H])
        for j in range(NSUB):
            spread_rows(rowc, j, 16, zz[:, sub(j)])

        out = jnp.zeros((RC, 128), F32)
        dcontrib = jnp.zeros((RC, SAMP), F32)
        for c in range(3):
            color = sigmoid(ray_row(rowc, 1 + c, 16) + smalls[5:6, TAIL + 1 + c : TAIL + 2 + c])
            out = out + jnp.where(lane128 == c, jnp.sum(contrib * color, axis=1, keepdims=True), 0.0)
            dcontrib = dcontrib + ccol[c] * color
            dlogit = ccol[c] * contrib * color * (1.0 - color)
            dzr[pl.ds(1 + c, RC, stride=16), :] = dlogit
            vac[2 + c] += dlogit
        weighted = dcontrib * contrib
        after_sum = exact(weighted, (iota((SAMP, SAMP), 0) > iota((SAMP, SAMP), 1)).astype(F32))
        dratio = (dcontrib * through - after_sum / factor) * ratio_d
        base = 1.0 / (before + 1e-05)
        dbefore = dratio * after * base * base * before * (1.0 - before)
        dafter = -dratio * base * after * (1.0 - after)
        dsigned = (dbefore + dafter) * inv_s
        dhalf = (dafter - dbefore) * inv_s
        vac[0] += dbefore * (signed - half) + dafter * (signed + half)
        vac[1] += dsigned
        dzr[pl.ds(0, RC, stride=16), :] = dsigned
        ddelta = dhalf * slope * 0.5
        dcosine = dhalf * delta * 0.5 * slope_d
        for j in range(NSUB):
            dzb[:, sub(j)] = gather_rows(dzr, 0, j, 16).astype(BF)

        zc[3] = nn(wcl[...], dzb[:, 0:PTS]).astype(BF) * dc[3]
        for l in range(3, 0, -1):
            zc[l - 1] = nn(w[5 + l], zc[l]).astype(BF) * dc[l - 1]
            acc[5 + l] += nt(hc[l - 1], zc[l])
            if last and l == 2:
                reduction.begin(0, grad_of(7), grad_of(8))
        dd = nn(wcx[...], zc[0]).astype(BF).astype(F32)
        for j in range(NSUB):
            spread_rows(dx, j, EROWS, dd[:, sub(j)])
        accx[...] += nt(fx[...], zc[0])
        accl[0] += nt(dzb[:, 0:PTS], hc[3, 0:H])
        fx[0:H] = nn(w[10], zc[0]).astype(BF)
        if last:
            reduction.begin(1, grad_of(6), turned(accx[0:H].astype(BF)))

        dpoint, dview = [], []
        for c in range(3):
            nb = ray_row(dx, 30 + c, EROWS) + dcosine * dcol[c]
            p = ray_row(dx, c, EROWS)
            v = ray_row(dx, 3 + c, EROWS) + dcosine * normal[c]
            eb[pl.ds(c, RC, stride=EROWS), :] = nb
            for k in range(6):
                two = 2.0**k
                sn, cs = feature(3 + 6 * k + c), feature(6 + 6 * k + c)
                eb[pl.ds(3 + 6 * k + c, RC, stride=EROWS), :] = two * cs * nb
                eb[pl.ds(6 + 6 * k + c, RC, stride=EROWS), :] = -two * sn * nb
                p = p - (two * two) * nb * (
                    sn * ray_row(de, 3 + 6 * k + c, EROWS) + cs * ray_row(de, 6 + 6 * k + c, EROWS)
                )
            for k in range(4):
                sn = xt[pl.ds(e0 + 6 + 6 * k + c, RC, stride=EROWS), :]
                cs = xt[pl.ds(e0 + 9 + 6 * k + c, RC, stride=EROWS), :]
                v = v + 2.0**k * (
                    cs * ray_row(dx, 6 + 6 * k + c, EROWS) - sn * ray_row(dx, 9 + 6 * k + c, EROWS)
                )
            dpoint.append(p)
            dview.append(v)

        for j in range(NSUB):
            encb[:, sub2(j)] = gather_rows(eb, 0, j, EROWS).astype(BF)
        for l in range(7):
            if l == 0:
                gg = nn(w0t[...], encb[:, PTS:])
            else:
                gg = nn(wt[l - 1], hx[l - 1, 0:H, PTS:])
            for j in range(NSUB):
                g = gg[:, sub(j)]
                s = ss[l, :, sub(j)]
                if l == 3:
                    g = g * s.astype(F32)
                    x = g.astype(BF)
                else:
                    x = g.astype(BF) * s
                u = wide(w7s[...]).astype(BF) if l == 6 else us[l, :, sub(j)]
                ts[l, :, sub(j)] = x * u * (2.0 - 2.0 * s)
                if l == 3:
                    e = gather_rows(eb, 0, j, EROWS)
                    x = ROOT_HALF * jnp.concatenate([g[0:EROWS] + e, g[EROWS:]], axis=0)
                    x = x.astype(BF)
                hx[l, 0:H, sub2(j)] = x
            if last and l in (3, 6):
                reduction.step_a(0 if l == 3 else 1)

        dd = nn(w[9], fx[0:H])
        for j in range(NSUB):
            row = gather_rows(dzr, 0, j, 16)[0:1]
            d = dd[:, sub(j)] + wide(w7s[...]) * row
            zg[6, :, sub(j)] = d.astype(BF) * ss[6, :, sub(j)] + ts[6, :, sub(j)]
        acc[9] += nt(hx[6, :, 0:PTS], fx[0:H])
        accl[1] += nt(dzb[...], hx[6, 0:H])
        for l in range(6, 0, -1):
            dd = nn(w[l - 1], zg[l, :, 0:PTS])
            for j in range(NSUB):
                d = dd[:, sub(j)].astype(BF)
                if l == 4:
                    d = d.astype(F32) * ROOT_HALF
                    spread_rows(dx, j, EROWS, d)
                    d = d.astype(BF)
                zg[l - 1, :, sub(j)] = d * ss[l - 1, :, sub(j)] + ts[l - 1, :, sub(j)]
            acc[l - 1] += nt(hx[l - 1], zg[l])
            if last and l == 6:
                reduction.begin(2, acc[9, 0:H], grad_of(5))
                reduction.step_b(0)
            elif last and l == 4:
                reduction.begin(3, grad_of(4), grad_of(3))
                reduction.step_a(2)
                reduction.step_b(1)
            elif last and l == 3:
                reduction.step_z(0)
            elif last and l == 2:
                reduction.begin(4, acc[2, 0:H], grad_of(1))
                reduction.step_a(3)
                reduction.step_b(2)
                reduction.step_z(1)
        acc0[...] += nt(encb[...], zg[0])
        if last:
            finish_weights()
        dd = nn(w0[...], zg[0, :, 0:PTS]).astype(BF).astype(F32)
        for j in range(NSUB):
            spread_rows(dx, j, EROWS, dd[:, sub(j)] + gather_rows(dx, 0, j, EROWS))

        depth = dep[pl.ds(r0, RC), :]
        ddepth = jnp.zeros((RC, SAMP), F32)
        for c in range(3):
            p = dpoint[c] + ray_row(dx, c, EROWS)
            for k in range(6):
                p = p + 2.0**k * (
                    feature(6 + 6 * k + c) * ray_row(dx, 3 + 6 * k + c, EROWS)
                    - feature(3 + 6 * k + c) * ray_row(dx, 6 + 6 * k + c, EROWS)
                )
            ddepth = ddepth + p * dcol[c]
            v = dview[c] + depth * p
            out = out + jnp.where(lane128 == 3 + c, jnp.sum(p, axis=1, keepdims=True), 0.0)
            out = out + jnp.where(lane128 == 6 + c, jnp.sum(v, axis=1, keepdims=True), 0.0)
        outc[pl.ds(r0, RC), :] = out
        later = exact(ddepth, (iota((SAMP, SAMP), 0) >= iota((SAMP, SAMP), 1)).astype(F32))
        deltag_o[pl.ds(r0, RC), :] = ddelta + later - 0.5 * ddepth

    total = Total(place, tc, ta, tb, tz, town, tsend, trecv)

    def finish_weights():
        tail_rows = jnp.where(row8 == 0, accl[1, 0:8], accl[0, 0:8])
        lines = [acc[0, H : H + 1]]
        for k in (0, 1, 4, 5, 3, 0, 6, 7, 8):
            lines.append(acc[k, H : H + 1])
        small_rows = jnp.concatenate(lines, axis=0)
        upper = jnp.concatenate(
            [
                acc0[...],
                jnp.zeros((CROSS - EROWS, H), F32),
                accx[H : H + EROWS],
                jnp.zeros((BIASES - CROSS - EROWS, H), F32),
                small_rows,
                jnp.zeros((TAIL - BIASES - 10, H), F32),
                tail_rows,
                jnp.zeros((H - TAIL - 8, H), F32),
            ],
            axis=0,
        )
        packed = turned(upper.astype(BF))
        reduction.begin(5, grad_of(0), packed)

        def amount(k):
            return jnp.sum(jnp.sum(vac[k], axis=1, keepdims=True), axis=0, keepdims=True)

        lane_bias = jnp.zeros((1, H), F32)
        for k in range(4):
            lane_bias = lane_bias + jnp.where(lane256 == TAIL + k, amount(1 + k), 0.0)
        variance = jnp.where(lane256 == 0, amount(0) * inv_s * 10.0, 0.0)
        sums = jnp.concatenate(
            [
                jnp.sum(d3 * acc[2, 0:H], axis=0, keepdims=True),
                acc[2, H : H + 1],
                jnp.sum(d7 * acc[9, 0:H], axis=0, keepdims=True),
                acc[9, H : H + 1],
                jnp.sum(misc * packed, axis=0, keepdims=True),
                lane_bias,
                variance,
                jnp.zeros((1, H), F32),
            ],
            axis=0,
        )
        total.begin(sums)

    each(0, rays // RC - 1, lambda i: chunk(i, False))
    chunk(rays // RC - 1, True)

    reduction.step_a(4)
    reduction.step_b(3)
    reduction.step_z(2)
    reduction.step_a(5)
    total.go_on(0)
    reduction.step_b(4)
    reduction.step_z(3)
    result = outc[...].T
    rgb_o[...] = result[0:3, 0:rays]
    ag_o[...] = result[3:6, 0:rays]
    dg_o[...] = result[6:9, 0:rays]
    total.go_on(1)
    reduction.step_b(5)
    reduction.step_z(4)
    total.go_on(2)
    reduction.step_z(5)
    for q in range(5):
        reduction.step_end(q)
    tot_o[...] = total.end()
    reduction.step_end(5)
    for q in range(6):
        reduction.settle(q)


def compute(fsdp, devices, anchors, directions, deltas, foreground, cotangent, smalls, layers):
    rays = deltas.shape[0]
    vm, dma = pltpu.VMEM, pltpu.SemaphoreType.DMA
    rp = layers[0].shape[0]
    points = rays * EROWS
    RC = 8 if devices <= 32 else 4
    PTS = RC * SAMP
    depth = fsdp // 2
    scratch = [
        vm((6, devices, 2 * rp, H), BF),
        vm((4, rp, 384), F32),
        dma((2, devices)),
        dma((2, devices)),
        vm((6, 2, 2 * depth, 2 * rp, H), BF),
        vm((6, 2 * depth, 2 * rp, H), BF),
        vm((6, depth, 2 * rp, H), BF),
        vm((6, depth, 2 * rp, H), BF),
        dma((6, 3 + depth)),
        dma((6, 2)),
        dma((6,)),
        dma((6,)),
        dma((6, depth)),
        vm((8, H), F32),
        vm((8, H), F32),
        vm((8, H), F32),
        vm((depth, 8, H), F32),
        vm((3, 8, H), F32),
        dma((2 + depth,)),
        dma((2 + depth,)),
        vm((GROUPS, H, H), BF),
        vm((8, 384), F32),
        vm((9, H, H), BF),
        vm((11, H, H), BF),
        vm((H + 16, H), BF),
        vm((H, EROWS), BF),
        vm((EROWS, H), BF),
        vm((H, H + EROWS), BF),
        vm((EROWS, H), BF),
        vm((16, H), BF),
        vm((H, 16), BF),
        vm((H, 128), F32),
        vm((10, H, 128), F32),
        vm((points, SAMP), F32),
        vm((ENC, rays, SAMP), F32),
        vm((points, SAMP), F32),
        vm((rays, SAMP), F32),
        vm((128, 128), F32),
        vm((7, H + 16, 2 * PTS), BF),
        vm((7, H, PTS), BF),
        vm((6, H, PTS), BF),
        vm((7, H, 2 * PTS), BF),
        vm((7, H, PTS), BF),
        vm((H + EROWS, PTS), BF),
        vm((4, H + 16, PTS), BF),
        vm((4, H, PTS), BF),
        vm((4, H, PTS), BF),
        vm((EROWS, 2 * PTS), BF),
        vm((16, 2 * PTS), BF),
        vm((RC * EROWS, SAMP), F32),
        vm((RC * EROWS, SAMP), F32),
        vm((RC * 16, SAMP), F32),
        vm((RC * 16, SAMP), F32),
        vm((RC * 16, SAMP), F32),
        vm((RC * EROWS, SAMP), F32),
        vm((RC * EROWS, SAMP), F32),
        vm((128, 128), F32),
        vm((10, H + 16, H), F32),
        vm((EROWS, H), F32),
        vm((H + EROWS, H), F32),
        vm((2, 16, H), F32),
        vm((5, RC, SAMP), F32),
    ]
    shapes = (
        jax.ShapeDtypeStruct((3, rays), F32),
        jax.ShapeDtypeStruct((3, rays), F32),
        jax.ShapeDtypeStruct((3, rays), F32),
        jax.ShapeDtypeStruct((rays, SAMP), F32),
        jax.ShapeDtypeStruct((GROUPS * rp, H), F32),
        jax.ShapeDtypeStruct((8, H), F32),
        jax.ShapeDtypeStruct((8, H), F32),
        jax.ShapeDtypeStruct((8, H), F32),
    )
    whole = pl.BlockSpec(memory_space=pltpu.VMEM)
    return pl.pallas_call(
        functools.partial(compute_kernel, fsdp, RC),
        out_shape=shapes,
        in_specs=[whole] * 30,
        out_specs=(whole,) * 8,
        scratch_shapes=scratch,
        name="nets",
        compiler_params=pltpu.CompilerParams(
            collective_id=0, has_side_effects=True, vmem_limit_bytes=62 * 1024 * 1024
        ),
    )(anchors, directions, deltas, foreground, cotangent, *smalls, *layers)


def unscaled_rows(d, gain, grad):
    inv = lax.rsqrt(jnp.sum(d * d, axis=1, keepdims=True) + EPS)
    dot = jnp.sum(d * grad, axis=1, keepdims=True)
    return grad * (gain * inv) - d * (gain * inv * inv * inv * dot), dot * inv


def finish_kernel(
    share, tot, inv, smalls, first, mid, narrow, skip, last, cfirst, cmid,
    fg, mg, sg, cg, cmg, cl, rgb, ag, dg, deltag, o_rgb, o_ag, o_dg, o_deltag,
    o_first, o_fg, o_fb, o_mid, o_mg, o_mb, o_narrow, o_ng, o_nb, o_skip, o_sg, o_sb,
    o_last, o_lg, o_lb, o_cfirst, o_cg, o_cb, o_cmid, o_cmg, o_cmb, o_clast, o_clg, o_clb, o_var,
    wid,
):
    r = first.shape[0]
    for src, dst in ((rgb, o_rgb), (ag, o_ag), (dg, o_dg), (deltag, o_deltag)):
        dst[...] = src[...]
    d_first, d_narrow, d_last, d_cfirst = share_rows(first, narrow, last, cfirst, wid)

    def vec(ref, k=None):
        return column(as_row(ref) if k is None else ref[...].astype(F32)[k : k + 1])

    def group(k):
        at = [g for pair in PAIRS for g in pair].index(k)
        return share[at * r : (at + 1) * r, :]

    def put(ref, col):
        ref[...] = line(col).reshape(r)

    def put_rows(ref, columns):
        ref[...] = jnp.concatenate([line(col) for col in columns], axis=0)

    misc = group(9)
    lane = iota((1, 128), 1)
    g, gain = unscaled_rows(d_first, vec(fg), jnp.where(lane < ENC, misc[:, 0:128], 0.0))
    o_first[...] = g[:, 0:ENC]
    put(o_fg, gain)
    put(o_fb, misc[:, ENC : ENC + 1])
    gains = []
    for k in range(4):
        g, gain = unscaled_rows(mid[k].astype(F32), vec(mg, k), group(k))
        o_mid[k] = g
        gains.append(gain)
    put_rows(o_mg, gains)
    put_rows(o_mb, [misc[:, BIASES + 1 + k : BIASES + 2 + k] for k in range(4)])
    g, gain = unscaled_rows(skip[...].astype(F32), vec(sg), pltpu.roll(group(4), H - ENC, 1))
    o_skip[...] = g
    put(o_sg, gain)
    put(o_sb, misc[:, BIASES + 5 : BIASES + 6])
    extra = jnp.where(lane < NX, misc[:, 128:256], 0.0)
    moved = jnp.concatenate([group(8), jnp.zeros((r, 128), F32)], axis=1)
    grad = pltpu.roll(moved, NX, 1) + jnp.concatenate([extra, jnp.zeros((r, H), F32)], axis=1)
    g, gain = unscaled_rows(d_cfirst, vec(cg), grad)
    o_cfirst[...] = g[:, 0 : H + NX]
    put(o_cg, gain)
    put(o_cb, misc[:, CROSS + NX : CROSS + NX + 1])
    gains = []
    for k in range(3):
        g, gain = unscaled_rows(cmid[k].astype(F32), vec(cmg, k), group(5 + k))
        o_cmid[k] = g
        gains.append(gain)
    put_rows(o_cmg, gains)
    put_rows(o_cmb, [misc[:, BIASES + 7 + k : BIASES + 8 + k] for k in range(3)])

    def across(k, d, grad):
        gain, iv, dot = smalls[k : k + 1, :], inv[k : k + 1, :], tot[k : k + 1, :]
        return grad * (gain * iv) - d * (gain * iv * iv * iv * dot)

    g = across(0, pltpu.roll(d_narrow, ENC, 1), group(10))
    o_narrow[...] = pltpu.roll(g, H - ENC, 1)[:, 0:NARROW]
    g = across(2, pltpu.roll(d_last, 383, 1)[:, 0:H], group(11))
    right = jnp.where(lane == TAIL - 128, d_last[:, 0:1], 0.0)
    for c in range(3):
        right = right + jnp.where(lane == TAIL - 127 + c, vec(cl, c), 0.0)
    t = across(4, jnp.concatenate([jnp.zeros((r, 128), F32), right], axis=1), misc)
    first_lane = iota((1, 384), 1) == 0

    def behind(x, front):
        more = jnp.zeros((x.shape[0], 128), F32)
        moved = pltpu.roll(jnp.concatenate([x, more], axis=1), 1, 1)
        return jnp.where(first_lane, front, moved)[:, 0 : H + 1]

    o_last[...] = behind(g, t[:, TAIL : TAIL + 1])
    put_rows(o_clast, [t[:, TAIL + 1 + c : TAIL + 2 + c] for c in range(3)])
    gained = tot[...] * inv[...]
    back = pltpu.roll(jnp.concatenate([gained[0:1], tot[1:2], jnp.zeros((6, H), F32)], axis=0), H - ENC, 1)
    o_ng[...] = back[0:1, 0:NARROW].reshape(NARROW)
    o_nb[...] = back[1:2, 0:NARROW].reshape(NARROW)
    eight = jnp.zeros((7, H), F32)
    o_lg[...] = behind(jnp.concatenate([gained[2:3], eight], axis=0), gained[4:5, TAIL : TAIL + 1])[0:1].reshape(H + 1)
    o_lb[...] = behind(jnp.concatenate([tot[3:4], eight], axis=0), tot[5:6, TAIL : TAIL + 1])[0:1].reshape(H + 1)
    tails = jnp.concatenate([gained[4:5], tot[5:6], jnp.zeros((6, H), F32)], axis=0)
    tails = pltpu.roll(tails, H - TAIL - 1, 1)
    o_clg[...] = tails[0:1, 0:3].reshape(3)
    o_clb[...] = tails[1:2, 0:3].reshape(3)
    o_var[...] = tot[6:7, 0:1].reshape(1)


def per_device(
    fsdp, devices,
    anchors, directions, deltas, foreground,
    sdf_first_dir, sdf_first_gain, sdf_first_bias,
    sdf_mid_dir, sdf_mid_gain, sdf_mid_bias,
    sdf_narrow_dir, sdf_narrow_gain, sdf_narrow_bias,
    sdf_skip_dir, sdf_skip_gain, sdf_skip_bias,
    sdf_last_dir, sdf_last_gain, sdf_last_bias,
    color_first_dir, color_first_gain, color_first_bias,
    color_mid_dir, color_mid_gain, color_mid_bias,
    color_last_dir, color_last_gain, color_last_bias,
    variance, rgb_cotangent,
):
    r = sdf_first_gain.shape[0]
    rp = max(r, 8)
    whole = pl.BlockSpec(memory_space=pltpu.VMEM)

    def rows(x):
        return x if rp == r else jnp.pad(x, [(0, 0)] * (x.ndim - 2) + [(0, rp - r), (0, 0)])

    def lanes(x):
        return x if rp == r else jnp.pad(x, [(0, 0)] * (x.ndim - 1) + [(0, rp - r)])

    shares = (
        rows(sdf_first_dir.T),
        rows(jnp.swapaxes(sdf_mid_dir, 1, 2)),
        rows(sdf_narrow_dir),
        rows(sdf_skip_dir.T),
        rows(sdf_last_dir),
        rows(color_first_dir.T),
        rows(jnp.swapaxes(color_mid_dir, 1, 2)),
    )
    fg, fb, mg, mb, sg, sb, cg, cb, cmg, cmb, cl = (
        lanes(x)
        for x in (
            sdf_first_gain, sdf_first_bias, sdf_mid_gain, sdf_mid_bias, sdf_skip_gain, sdf_skip_bias,
            color_first_gain, color_first_bias, color_mid_gain, color_mid_bias, color_last_dir.T,
        )
    )
    rgb, ag, dg, deltag, share, tot, inv, smalls = compute(
        fsdp, devices, anchors, directions, deltas, foreground, rgb_cotangent,
        (
            variance, sdf_narrow_gain, sdf_narrow_bias, sdf_last_gain, sdf_last_bias,
            color_last_gain, color_last_bias,
        ),
        (*shares, fg, fb, mg, mb, sg, sb, cg, cb, cmg, cmb, cl),
    )
    def f32(*shape):
        return jax.ShapeDtypeStruct(shape, F32)

    outs = pl.pallas_call(
        finish_kernel,
        out_shape=(
            f32(*rgb.shape), f32(*ag.shape), f32(*dg.shape), f32(*deltag.shape),
            f32(rp, ENC), f32(rp), f32(rp),
            f32(4, rp, H), f32(4, rp), f32(4, rp),
            f32(rp, NARROW), f32(NARROW), f32(NARROW),
            f32(rp, H), f32(rp), f32(rp),
            f32(rp, H + 1), f32(H + 1), f32(H + 1),
            f32(rp, H + NX), f32(rp), f32(rp),
            f32(3, rp, H), f32(3, rp), f32(3, rp),
            f32(3, rp), f32(3), f32(3),
            f32(1),
        ),
        in_specs=[whole] * 21,
        out_specs=(whole,) * 29,
        scratch_shapes=[pltpu.VMEM((4, rp, 384), F32)],
        name="finish",
    )(share, tot, inv, smalls, *shares, fg, mg, sg, cg, cmg, cl, rgb, ag, dg, deltag)
    (
        rgb, ag, dg, deltag,
        o_first, o_fg, o_fb, o_mid, o_mg, o_mb, o_narrow, o_ng, o_nb, o_skip, o_sg, o_sb,
        o_last, o_lg, o_lb, o_cfirst, o_cg, o_cb, o_cmid, o_cmg, o_cmb, o_clast, o_clg, o_clb, o_var,
    ) = outs
    return (
        rgb, ag, dg, deltag,
        o_first[0:r].T, o_fg[0:r], o_fb[0:r],
        jnp.swapaxes(o_mid[:, 0:r], 1, 2), o_mg[:, 0:r], o_mb[:, 0:r],
        o_narrow[0:r], o_ng, o_nb,
        o_skip[0:r].T, o_sg[0:r], o_sb[0:r],
        o_last[0:r], o_lg, o_lb,
        o_cfirst[0:r].T, o_cg[0:r], o_cb[0:r],
        jnp.swapaxes(o_cmid[:, 0:r], 1, 2), o_cmg[:, 0:r], o_cmb[:, 0:r],
        o_clast[:, 0:r].T, o_clg, o_clb,
        o_var,
    )


def solution(mesh):
    fsdp, rep = mesh.shape["fsdp"], mesh.shape["rep"]
    assert rep == 4 and fsdp % 2 == 0
    both = ("fsdp", "rep")
    cols, vec, cols3, rows, copied = P(None, both), P(both), P(None, None, both), P(both, None), P()
    layers = (
        cols, vec, vec, cols3, cols, cols, rows, copied, copied, cols, vec, vec,
        rows, copied, copied, cols, vec, vec, cols3, cols, cols, rows, copied, copied,
    )
    return jax.shard_map(
        functools.partial(per_device, fsdp, fsdp * rep),
        mesh=mesh,
        in_specs=(cols, cols, rows, rows) + layers + (copied, cols),
        out_specs=(cols, cols, cols, rows) + layers + (copied,),
        check_vma=False,
    )
```

```python
import functools

import jax
import jax.numpy as jnp
from jax import lax
from jax.experimental import pallas as pl
from jax.experimental.pallas import tpu as pltpu
from jax.sharding import PartitionSpec as P

F32 = jnp.float32
BF = jnp.bfloat16
H = 256
SAMP = 128
ENC = 39
EROWS = 48
NARROW = 217
NX = 33
GROUPS = 12
SUB = 256
PAIRS = ((6, 7), (5, 8), (11, 3), (2, 4), (10, 1), (0, 9))
RSUB = SUB // SAMP
CROSS = 128
BIASES = 200
TAIL = 216
TOT = 24
EPS = 1e-06
HALF_LN2 = 0.34657359027997264
ROOT_HALF = 0.7071067811865476


def nn(a, b):
    return lax.dot_general(a, b, (((1,), (0,)), ((), ())), preferred_element_type=F32)


def nt(a, b):
    return lax.dot_general(a, b, (((1,), (1,)), ((), ())), preferred_element_type=F32)


def exact(a, b):
    return lax.dot_general(
        a, b, (((1,), (0,)), ((), ())), precision=lax.Precision.HIGHEST, preferred_element_type=F32
    )


def iota(shape, dim):
    return lax.broadcasted_iota(jnp.int32, shape, dim)


def column(row):
    n = row.shape[1]
    return jnp.sum(jnp.where(iota((n, n), 0) == iota((n, n), 1), row, 0.0), axis=1, keepdims=True)


def as_row(ref):
    return ref[...].astype(F32).reshape(1, ref.shape[0])


def line(col):
    n = col.shape[0]
    return jnp.sum(jnp.where(iota((n, n), 0) == iota((n, n), 1), col, 0.0), axis=0, keepdims=True)


def wide(half):
    return jnp.concatenate([half, half], axis=1)


def sharp(z):
    s = 0.5 * jnp.tanh(z) + 0.5
    return jnp.maximum(z, 0.0) - 0.5 * jnp.log(jnp.maximum(s, 1.0 - s)), s


def silu(z):
    g = 0.5 * jnp.tanh(0.5 * z) + 0.5
    h = z * g
    return h, g + h * (1.0 - g)


def softplus(x):
    return jnp.maximum(x, 0.0) + jnp.log(1.0 + jnp.exp(-jnp.abs(x)))


def sigmoid(x):
    return 1.0 / (1.0 + jnp.exp(-x))


def scaled_rows(d, gain):
    return d * (gain * lax.rsqrt(jnp.sum(d * d, axis=1, keepdims=True) + EPS))


def share_rows(first, narrow, last, cfirst, wid):
    r = first.shape[0]

    def padded(k, ref, lanes):
        wid[k] = jnp.zeros(wid.shape[1:], F32)
        wid[k, :, 0 : ref.shape[1]] = ref[...].astype(F32)
        return wid[k][:, 0:lanes]

    return (padded(0, first, 128), padded(1, narrow, H), padded(2, last, 384), padded(3, cfirst, 384))


class Place:
    def __init__(self, fsdp):
        f, p = lax.axis_index("fsdp"), lax.axis_index("rep")
        self.depth = fsdp // 2
        self.z, self.y, self.x, self.c = f // 2, f % 2, p // 2, p % 2

    def at(self, half, z, a=0, b=0, c=0):
        dy, dx = (a, b) if half == 0 else (b, a)
        return z, (self.y + dy) % 2, (self.x + dx) % 2, (self.c + c) % 2

    def index(self, *where):
        z, y, x, c = self.at(*where)
        return ((z * 2 + y) * 2 + x) * 2 + c

    def device(self, *where):
        z, y, x, c = self.at(*where)
        return z * 2 + y, x * 2 + c

    def turn(self, k):
        return (self.z + k) % self.depth

    def greet(self, barrier):
        def one(k, carry):
            signal(barrier, self.device(0, self.turn(k)))
            return carry

        lax.fori_loop(1, self.depth, one, 0)
        for flips in ((1, 0, 0), (0, 1, 0), (0, 0, 1)):
            signal(barrier, self.device(0, self.z, *flips))

    def wait_all(self, barrier):
        pl.semaphore_wait(barrier, self.depth + 2)


def signal(sem, device):
    pl.semaphore_signal(sem, inc=1, device_id=device, device_id_type=pl.DeviceIdType.MESH)


def remote(src, dst, send, recv, device):
    return pltpu.make_async_remote_copy(
        src_ref=src, dst_ref=dst, send_sem=send, recv_sem=recv,
        device_id=device, device_id_type=pl.DeviceIdType.MESH,
    )


def each(start, stop, body):
    def one(k, carry):
        body(k)
        return carry

    lax.fori_loop(start, stop, one, 0)


def own_share(
    first, mid, narrow, skip, last, cfirst, cmid, fg, fb, mg, mb, sg, sb, cg, cb, cmg, cmb, cl, wid
):
    d_first, d_narrow, d_last, d_cfirst = share_rows(first, narrow, last, cfirst, wid)

    def vec(ref, k=None):
        row = as_row(ref) if k is None else ref[...].astype(F32)[k : k + 1]
        return column(row)

    lane = iota((1, 128), 1)
    parts = [scaled_rows(mid[k].astype(F32), vec(mg, k)) for k in range(4)]
    parts.append(pltpu.roll(scaled_rows(skip[...].astype(F32), vec(sg)), ENC, 1))
    parts += [scaled_rows(cmid[k].astype(F32), vec(cmg, k)) for k in range(3)]
    s_cfirst = scaled_rows(d_cfirst, vec(cg))
    parts.append(pltpu.roll(s_cfirst, 384 - NX, 1)[:, 0:H])
    left = scaled_rows(d_first, vec(fg)) + jnp.where(lane == ENC, vec(fb), 0.0)
    right = jnp.where(lane < NX, s_cfirst[:, 0:128], 0.0) + jnp.where(lane == NX, vec(cb), 0.0)
    biases = [(1, mb, 0), (2, mb, 1), (3, mb, 2), (4, mb, 3), (5, sb, None), (7, cmb, 0), (8, cmb, 1), (9, cmb, 2)]
    for j, ref, k in biases:
        right = right + jnp.where(lane == BIASES - 128 + j, vec(ref, k), 0.0)
    right = right + jnp.where(lane == TAIL - 128, d_last[:, 0:1], 0.0)
    for c in range(3):
        right = right + jnp.where(lane == TAIL - 127 + c, vec(cl, c), 0.0)
    parts.append(jnp.concatenate([left, right], axis=1))
    parts.append(pltpu.roll(d_narrow, ENC, 1))
    parts.append(pltpu.roll(d_last, 383, 1)[:, 0:H])
    return [jnp.concatenate([parts[k] for k in pair], axis=0).astype(BF) for pair in PAIRS]


def gather(place, out, send, recv, meanwhile):
    z, depth = place.z, place.depth
    me = place.index(0, z)
    def copy(half, slab, s, *to):
        part = out.at[pl.ds(half * 3, 3), slab]
        return remote(part, part, send.at[half, s], recv.at[half, slab], place.device(half, *to))

    def arrived(half, slab):
        copy(half, slab, 0, z, 0, 0, 1).wait_recv()

    def along_z(k):
        for half in range(2):
            copy(half, me, k - 1, place.turn(k)).start()

    def pass_on(half, slab, t, stage):
        base = depth - 1
        if stage == 0:
            copy(half, slab, base + t, z, 1).start()
        if stage <= 1:
            copy(half, slab, base + depth + 2 * t + stage, z, 0, 1).start()
        copy(half, slab, base + 3 * depth + 4 * t + stage, z, 0, 0, 1).start()

    each(1, depth, along_z)
    for half in range(2):
        pass_on(half, me, 0, 0)

    def from_z(k):
        for half in range(2):
            slab = place.index(half, place.turn(k))
            arrived(half, slab)
            pass_on(half, slab, k, 0)

    def from_a(k):
        for half in range(2):
            slab = place.index(half, place.turn(k), 1)
            arrived(half, slab)
            pass_on(half, slab, k, 1)

    def from_b(k):
        for half in range(2):
            slab = place.index(half, place.turn(k), 0, 1)
            arrived(half, slab)
            pass_on(half, slab, k, 2)

    def from_ab(k):
        for half in range(2):
            slab = place.index(half, place.turn(k), 1, 1)
            arrived(half, slab)
            pass_on(half, slab, k, 3)

    def from_core(k):
        for half in range(2):
            for a in range(2):
                for b in range(2):
                    arrived(half, place.index(half, place.turn(k), a, b, 1))

    def sent(s):
        for half in range(2):
            copy(half, me, s, z, 0, 0, 1).wait_send()

    meanwhile()
    each(1, depth, from_z)
    each(0, depth, from_a)
    each(0, depth, from_b)
    each(0, depth, from_ab)
    each(0, depth, from_core)
    each(0, 8 * depth - 1, sent)


class Reduction:
    def __init__(self, place, g, share, rcc, rca, rcb, rcz, send, sc, sa, sb, sz):
        self.place, self.g, self.share = place, g, share
        self.rcc, self.rca, self.rcb, self.rcz = rcc, rca, rcb, rcz
        self.send, self.sc, self.sa, self.sb, self.sz = send, sc, sa, sb, sz

    def side(self, q):
        place = self.place
        return (place.y, place.x) if q % 2 == 0 else (place.x, place.y)

    def to_core(self, q, t):
        n, place = 2 * self.place.depth, self.place
        at = ((place.c + 1) % 2) * 2 + (self.side(q)[0] + t) % 2
        return remote(
            self.g.at[q, pl.ds(at * n, n)], self.rcc.at[q, t], self.send.at[q, t], self.sc.at[q, t],
            place.device(q % 2, place.z, 0, 0, 1),
        )

    def to_a(self, q):
        return remote(
            self.rcc.at[q, 1], self.rca.at[q], self.send.at[q, 2], self.sa.at[q],
            self.place.device(q % 2, self.place.z, 1),
        )

    def to_b(self, q):
        n = self.place.depth
        at = (self.side(q)[1] + 1) % 2
        return remote(
            self.rca.at[q, pl.ds(at * n, n)], self.rcb.at[q], self.send.at[q, 3], self.sb.at[q],
            self.place.device(q % 2, self.place.z, 0, 1),
        )

    def to_z(self, q, k):
        to = self.place.turn(k)
        return remote(
            self.rcb.at[q, to], self.rcz.at[q, k], self.send.at[q, 3 + k], self.sz.at[q, k],
            self.place.device(0, to),
        )

    def begin(self, q, first, second):
        depth = self.place.depth
        count = depth * 8
        r, rp = H // count, self.g.shape[2] // 2
        for d in range(count):
            z, y, x, c = d // 8, d // 4 % 2, d // 2 % 2, d % 2
            a, b = (y, x) if q % 2 == 0 else (x, y)
            parts = []
            for m in (first, second):
                parts.append(m[d * r : (d + 1) * r])
                if rp > r:
                    parts.append(jnp.zeros((rp - r, H), F32))
            self.g[q, ((c * 2 + a) * 2 + b) * depth + z] = jnp.concatenate(parts, axis=0).astype(BF)
        self.to_core(q, 1).start()
        self.to_core(q, 0).start()

    def own(self, q, t):
        n = 2 * self.place.depth
        return self.g[q, pl.ds((self.place.c * 2 + (self.side(q)[0] + t) % 2) * n, n)].astype(F32)

    def step_a(self, q):
        self.to_core(q, 1).wait_recv()
        self.rcc[q, 1] = (self.rcc[q, 1].astype(F32) + self.own(q, 1)).astype(BF)
        self.to_a(q).start()
        self.to_core(q, 0).wait_recv()
        self.rcc[q, 0] = (self.rcc[q, 0].astype(F32) + self.own(q, 0)).astype(BF)

    def add_a(self, q, t):
        n = self.place.depth
        at = pl.ds(((self.side(q)[1] + t) % 2) * n, n)
        self.rca[q, at] = (self.rca[q, at].astype(F32) + self.rcc[q, 0, at].astype(F32)).astype(BF)

    def step_b(self, q):
        self.to_a(q).wait_recv()
        self.add_a(q, 1)
        self.to_b(q).start()
        self.add_a(q, 0)

    def step_z(self, q):
        n, z = self.place.depth, self.place.z
        self.to_b(q).wait_recv()
        at = pl.ds(self.side(q)[1] * n, n)
        self.rcb[q] = (self.rcb[q].astype(F32) + self.rca[q, at].astype(F32)).astype(BF)
        each(1, n, lambda k: self.to_z(q, k).start())
        rows = self.g.shape[2]
        self.share[q * rows : (q + 1) * rows] = self.rcb[q, z].astype(F32)

    def step_end(self, q):
        rows = self.g.shape[2]

        def one(k):
            self.to_z(q, k).wait_recv()
            self.share[q * rows : (q + 1) * rows] += self.rcz[q, k].astype(F32)

        each(1, self.place.depth, one)

    def settle(self, q):
        for t in range(2):
            self.to_core(q, t).wait_send()
        self.to_a(q).wait_send()
        self.to_b(q).wait_send()
        each(1, self.place.depth, lambda k: self.to_z(q, k).wait_send())


class Total:
    def __init__(self, place, tc, ta, tb, tz, own, send, recv):
        self.place, self.bufs, self.own = place, (tc, ta, tb), own
        self.tz, self.send, self.recv = tz, send, recv

    def step(self, k):
        to = ((0, 0, 1), (1, 0, 0), (0, 1, 0))[k]
        return remote(
            self.own.at[k], self.bufs[k], self.send.at[k], self.recv.at[k],
            self.place.device(0, self.place.z, *to),
        )

    def begin(self, value):
        self.own[0] = value
        self.step(0).start()

    def go_on(self, k):
        self.step(k).wait()
        value = self.own[k] + self.bufs[k][...]
        if k < 2:
            self.own[k + 1] = value
            self.step(k + 1).start()
        else:
            self.tz[self.place.z] = value
            each(1, self.place.depth, lambda k: self.along(k).start())

    def along(self, k):
        mine = self.tz.at[self.place.z]
        return remote(
            mine, mine, self.send.at[2 + k], self.recv.at[2 + k], self.place.device(0, self.place.turn(k))
        )

    def end(self):
        each(1, self.place.depth, lambda k: self.along(k).wait())
        total = self.tz[0]
        for k in range(1, self.place.depth):
            total = total + self.tz[k]
        return total


def compute_kernel(
    fsdp, rc, anch, dirs, delt, fore, cot, var, ng, nb, lg, lb, cg, cb, *rest
):
    layers, rest = rest[:18], rest[18:]
    compute_body(fsdp, rc, layers, anch, dirs, delt, fore, cot, var, ng, nb, lg, lb, cg, cb, *rest)


def compute_body(
    fsdp, RC, layers, anch, dirs, delt, fore, cot, var, ng, nb, lg, lb, cg, cb,
    rgb_o, ag_o, dg_o, deltag_o, share_o, tot_o, inv_o, smalls,
    gathered, wid, send, recv,
    rcc, rca, rcb, rcz, rsend, sc, sa, sb, sz, tc, ta, tb, tz, town, tsend, trecv, wts, sm, wt, w, wt7, w0t, w0, wcft, wcx, wclt, wcl, w7s, bb,
    enc, fe, xt, dep, cols,
    hx, ss, us, zg, ts, fx, hc, dc, zc, encb, dzb,
    de, nr, row7, rowc, dzr, dx, eb, outc,
    acc, acc0, accx, accl, vac,
):
    rays = delt.shape[0]
    PTS = RC * SAMP
    NSUB = PTS // SUB
    lane128 = iota((1, 128), 1)

    place = Place(fsdp)
    barrier = pltpu.get_barrier_semaphore()
    place.greet(barrier)
    for q, part in enumerate(own_share(*layers, wid)):
        gathered[q, place.index(0, place.z)] = part
    place.wait_all(barrier)

    def meanwhile():
        cols[...] = jnp.zeros(cols.shape, F32)
        cols[0:3, 0:rays] = anch[...]
        cols[3:6, 0:rays] = dirs[...]
        cols[6:9, 0:rays] = cot[...]
        percol = cols[...].T
        cols[...] = percol
        low = (iota((SAMP, SAMP), 0) <= iota((SAMP, SAMP), 1)).astype(F32)
        dall = delt[...]
        depth = 0.1 + exact(dall, low) - 0.5 * dall
        dep[...] = depth
        enc[...] = jnp.zeros(enc.shape, F32)
        xt[...] = jnp.zeros(xt.shape, F32)
        enc[pl.ds(ENC, rays, stride=EROWS), :] = jnp.ones((rays, SAMP), F32)
        xt[pl.ds(NX, rays, stride=EROWS), :] = jnp.ones((rays, SAMP), F32)

        def put_enc(f, value):
            fe[f] = value
            enc[pl.ds(f, rays, stride=EROWS), :] = value

        for c in range(3):
            view = jnp.broadcast_to(percol[0:rays, 3 + c : 4 + c], (rays, SAMP))
            p = percol[0:rays, c : c + 1] + depth * view
            put_enc(c, p)
            xt[pl.ds(c, rays, stride=EROWS), :] = p
            sn, cs = jnp.sin(p), jnp.cos(p)
            for k in range(6):
                put_enc(3 + 6 * k + c, sn)
                put_enc(6 + 6 * k + c, cs)
                sn, cs = 2.0 * sn * cs, 1.0 - 2.0 * sn * sn
            xt[pl.ds(3 + c, rays, stride=EROWS), :] = view
            sn, cs = jnp.sin(view), jnp.cos(view)
            for k in range(4):
                xt[pl.ds(6 + 6 * k + c, rays, stride=EROWS), :] = sn
                xt[pl.ds(9 + 6 * k + c, rays, stride=EROWS), :] = cs
                sn, cs = 2.0 * sn * cs, 1.0 - 2.0 * sn * sn

        nr[...] = jnp.zeros(nr.shape, F32)
        eb[...] = jnp.zeros(eb.shape, F32)
        dzr[...] = jnp.zeros(dzr.shape, F32)
        acc[...] = jnp.zeros(acc.shape, F32)
        acc0[...] = jnp.zeros(acc0.shape, F32)
        accx[...] = jnp.zeros(accx.shape, F32)
        accl[...] = jnp.zeros(accl.shape, F32)
        vac[...] = jnp.zeros(vac.shape, F32)
        hx[:, H : H + 16, 0:PTS] = jnp.ones((7, 16, PTS), BF)
        hx[:, H : H + 16, PTS:] = jnp.zeros((7, 16, PTS), BF)
        dzb[:, PTS:] = jnp.where(iota((16, PTS), 0) == 0, 1.0, 0.0).astype(BF)
        hc[:, H : H + 16, :] = jnp.ones((4, 16, PTS), BF)

    gather(place, gathered, send, recv, meanwhile)

    lane256 = iota((1, H), 1)
    sm[...] = jnp.zeros(sm.shape, F32)
    for k, ref in enumerate((ng, nb, lg, lb, cg, cb)):
        sm[k : k + 1, 0 : ref.shape[0]] = as_row(ref)
    near = pltpu.roll(sm[:, 0:H], H - NARROW, 1)
    tail_row = []
    for k in (0, 1):
        t = jnp.where(lane256 == TAIL, sm[2 + k : 3 + k, 0:1], 0.0)
        for c in range(3):
            t = t + jnp.where(lane256 == TAIL + 1 + c, sm[4 + k : 5 + k, c : c + 1], 0.0)
        tail_row.append(t)
    smalls[...] = jnp.concatenate(
        [
            near[0:1],
            near[1:2] + jnp.where(lane256 < ENC, -1e4, 0.0),
            pltpu.roll(sm[...], 383, 1)[2:4, 0:H],
            tail_row[0],
            tail_row[1],
            jnp.broadcast_to(as_row(var), (1, H)),
            jnp.zeros((1, H), F32),
        ],
        axis=0,
    )
    r = H // gathered.shape[1]
    rp = gathered.shape[2] // 2
    for q, groups in enumerate(PAIRS):
        pair = gathered[q].astype(F32)
        wts[groups[0]] = pair[:, 0:r].reshape(H, H).astype(BF)
        wts[groups[1]] = pair[:, rp : rp + r].reshape(H, H).astype(BF)

    unit = (iota((H, H), 0) == iota((H, H), 1)).astype(BF)

    def turned(x):
        return nt(unit, x)

    misc = wts[9].astype(F32)
    misct = turned(wts[9])
    for k, src in enumerate((0, 1, None, 4, 2, 3, 5, 6, 7)):
        if src is not None:
            wt[k] = wts[src]
            w[k] = turned(wts[src]).astype(BF)
    d3 = wts[10].astype(F32)
    inv3 = lax.rsqrt(jnp.sum(d3 * d3, axis=0, keepdims=True) + EPS)
    w3 = (d3 * (smalls[0:1, :] * inv3)).astype(BF)
    w[2] = w3
    wt[2] = turned(w3).astype(BF)
    d7 = wts[11].astype(F32)
    inv7 = lax.rsqrt(jnp.sum(d7 * d7, axis=0, keepdims=True) + EPS)
    w7 = (d7 * (smalls[2:3, :] * inv7)).astype(BF)
    w[9] = w7
    wt7[0:H] = turned(w7).astype(BF)
    w[10] = turned(wts[8]).astype(BF)
    invm = lax.rsqrt(jnp.sum(misc * misc, axis=0, keepdims=True) + EPS)
    tail = (misc * (smalls[4:5, :] * invm)).astype(BF)
    tailt = turned(tail)[TAIL : TAIL + 8]
    tail = tail.astype(F32)
    row8 = iota((8, H), 0)
    none8 = jnp.zeros((8, H), F32)
    wt7[H : H + 16] = jnp.concatenate([jnp.where(row8 == 0, tailt, 0.0), none8], axis=0).astype(BF)
    wclt[...] = jnp.concatenate(
        [jnp.where((row8 > 0) & (row8 < 4), tailt, 0.0), none8], axis=0
    ).astype(BF)
    only = jnp.where((lane256 > TAIL) & (lane256 < TAIL + 4), tail, 0.0)
    wcl[...] = pltpu.roll(only, H - TAIL, 1)[:, 0:16].astype(BF)
    w7s[...] = jnp.broadcast_to(tail[:, TAIL : TAIL + 1], (H, 128))
    w0t[...] = misc[:, 0:EROWS].astype(BF)
    w0[...] = misct[0:EROWS].astype(BF)
    wcx[...] = misct[CROSS : CROSS + EROWS].astype(BF)
    wcft[:, 0:H] = wts[8]
    wcft[:, H : H + EROWS] = misc[:, CROSS : CROSS + EROWS].astype(BF)
    for k, j in enumerate((1, 2, None, 5, 3, 4, None, 7, 8, 9)):
        if j is not None:
            bb[k] = jnp.broadcast_to(misc[:, BIASES + j : BIASES + j + 1], (H, 128))
    bb[2] = jnp.broadcast_to(column(smalls[1:2, :]), (H, 128))
    bb[6] = jnp.broadcast_to(column(smalls[3:4, :]), (H, 128))
    inv_o[...] = jnp.concatenate([inv3, inv3, inv7, inv7, invm, invm, invm, invm], axis=0)

    inv_s = jnp.exp(10.0 * smalls[6:7, 0:1])

    reduction = Reduction(place, gathered, share_o, rcc, rca, rcb, rcz, rsend, sc, sa, sb, sz)

    def grad_of(k):
        return turned(acc[k, 0:H].astype(BF))

    def chunk(i, last):
        if last:
            r0, e0 = i * RC, i * RC * EROWS
        else:
            r0 = pl.multiple_of(i * RC, RC)
            e0 = pl.multiple_of(i * (RC * EROWS), 8)

        def sub(j):
            return slice(j * SUB, (j + 1) * SUB)

        def sub2(j):
            return slice(PTS + j * SUB, PTS + (j + 1) * SUB)

        def gather_rows(ref, base, j, count):
            start = base + j * RSUB * count
            if not isinstance(start, int):
                start = pl.multiple_of(start, 8)
                return jnp.concatenate(
                    [ref[pl.ds(pl.multiple_of(start + t * count, 8), count), :] for t in range(RSUB)],
                    axis=1,
                )
            return jnp.concatenate(
                [ref[start + t * count : start + (t + 1) * count, :] for t in range(RSUB)], axis=1
            )

        def spread_rows(ref, j, count, value):
            for t in range(RSUB):
                at = (j * RSUB + t) * count
                ref[at : at + count, :] = value[0:count, t * SAMP : (t + 1) * SAMP]

        def ray_row(ref, f, count):
            return ref[pl.ds(f, RC, stride=count), :]

        for j in range(NSUB):
            encb[:, sub(j)] = gather_rows(enc, e0, j, EROWS).astype(BF)
        for l in range(7):
            if l == 0:
                zz = nn(w0t[...], encb[:, 0:PTS])
            else:
                zz = nn(wt[l - 1], hx[l - 1, 0:H, 0:PTS])
            for j in range(NSUB):
                z = zz[:, sub(j)]
                if l > 0:
                    z = z + wide(bb[l - 1])
                h, s = sharp(z)
                ss[l, :, sub(j)] = s
                if l == 3:
                    e = gather_rows(enc, e0, j, EROWS)
                    keep = iota((EROWS, 1), 0) < ENC
                    h = h.astype(F32)
                    h = ROOT_HALF * jnp.concatenate(
                        [h[0:EROWS] + jnp.where(keep, e, 0.0), h[EROWS:]], axis=0
                    )
                hx[l, 0:H, sub(j)] = h.astype(BF)
        zz = nn(wt7[...], hx[6, 0:H, 0:PTS])
        for j in range(NSUB):
            z = zz[:, sub(j)]
            fx[0:H, sub(j)] = (z[0:H] + wide(bb[6])).astype(BF)
            spread_rows(row7, j, 16, z[H : H + 16])

        for j in range(NSUB):
            zg[6, :, sub2(j)] = (wide(w7s[...]) * ss[6, :, sub(j)]).astype(BF)
        for l in range(6, 0, -1):
            uu = nn(w[l - 1], zg[l, :, PTS:])
            for j in range(NSUB):
                u = uu[:, sub(j)].astype(BF).astype(F32)
                if l == 4:
                    u = u * ROOT_HALF
                    spread_rows(de, j, EROWS, u)
                us[l - 1, :, sub(j)] = u.astype(BF)
                zg[l - 1, :, sub2(j)] = (u * ss[l - 1, :, sub(j)]).astype(BF)
        dd = nn(w0[...], zg[0, :, PTS:]).astype(BF).astype(F32)
        for j in range(NSUB):
            d = dd[:, sub(j)]
            spread_rows(de, j, EROWS, d + gather_rows(de, 0, j, EROWS))

        def feature(f):
            return fe[f, pl.ds(r0, RC), :]

        def ray_col(j):
            return jnp.broadcast_to(cols[pl.ds(r0, RC), j : j + 1], (RC, SAMP))

        dcol = [ray_col(3 + c) for c in range(3)]
        ccol = [ray_col(6 + c) for c in range(3)]
        normal = []
        for c in range(3):
            n = ray_row(de, c, EROWS)
            for k in range(6):
                n = n + 2.0**k * (
                    feature(6 + 6 * k + c) * ray_row(de, 3 + 6 * k + c, EROWS)
                    - feature(3 + 6 * k + c) * ray_row(de, 6 + 6 * k + c, EROWS)
                )
            normal.append(n)
            nr[pl.ds(30 + c, RC, stride=EROWS), :] = n

        delta = delt[pl.ds(r0, RC), :]
        front = fore[pl.ds(r0, RC), :].astype(F32)
        signed = ray_row(row7, 0, 16) + smalls[5:6, TAIL : TAIL + 1]
        cosine = dcol[0] * normal[0] + dcol[1] * normal[1] + dcol[2] * normal[2]
        slope = softplus(-10.0 * cosine) * -0.1
        slope_d = sigmoid(-10.0 * cosine)
        half = slope * delta * 0.5
        before = sigmoid((signed - half) * inv_s)
        after = sigmoid((signed + half) * inv_s)
        ratio = (before - after + 1e-05) / (before + 1e-05)
        ratio_d = front * (sigmoid(20.0 * ratio) - sigmoid(20.0 * (ratio - 1.0)))
        opacity = front * (softplus(20.0 * ratio) - softplus(20.0 * (ratio - 1.0))) * 0.05
        factor = 1.0 - opacity + 1e-07
        survive = factor
        lane = iota((RC, SAMP), 1)
        step = 1
        while step < SAMP:
            survive = survive * jnp.where(lane >= step, pltpu.roll(survive, step, 1), 1.0)
            step *= 2
        through = jnp.where(lane >= 1, pltpu.roll(survive, 1, 1), 1.0)
        contrib = opacity * through

        for j in range(NSUB):
            x = gather_rows(xt, e0, j, EROWS) + gather_rows(nr, 0, j, EROWS)
            fx[H : H + EROWS, sub(j)] = x.astype(BF)
        for l in range(4):
            if l == 0:
                zz = nn(wcft[...], fx[...])
            else:
                zz = nn(wt[5 + l], hc[l - 1, 0:H])
            for j in range(NSUB):
                z = zz[:, sub(j)]
                if l > 0:
                    z = z + wide(bb[6 + l])
                h, d = silu(z)
                hc[l, 0:H, sub(j)] = h.astype(BF)
                dc[l, :, sub(j)] = d.astype(BF)
        zz = nn(wclt[...], hc[3, 0:H])
        for j in range(NSUB):
            spread_rows(rowc, j, 16, zz[:, sub(j)])

        out = jnp.zeros((RC, 128), F32)
        dcontrib = jnp.zeros((RC, SAMP), F32)
        for c in range(3):
            color = sigmoid(ray_row(rowc, 1 + c, 16) + smalls[5:6, TAIL + 1 + c : TAIL + 2 + c])
            out = out + jnp.where(lane128 == c, jnp.sum(contrib * color, axis=1, keepdims=True), 0.0)
            dcontrib = dcontrib + ccol[c] * color
            dlogit = ccol[c] * contrib * color * (1.0 - color)
            dzr[pl.ds(1 + c, RC, stride=16), :] = dlogit
            vac[2 + c] += dlogit
        weighted = dcontrib * contrib
        after_sum = exact(weighted, (iota((SAMP, SAMP), 0) > iota((SAMP, SAMP), 1)).astype(F32))
        dratio = (dcontrib * through - after_sum / factor) * ratio_d
        base = 1.0 / (before + 1e-05)
        dbefore = dratio * after * base * base * before * (1.0 - before)
        dafter = -dratio * base * after * (1.0 - after)
        dsigned = (dbefore + dafter) * inv_s
        dhalf = (dafter - dbefore) * inv_s
        vac[0] += dbefore * (signed - half) + dafter * (signed + half)
        vac[1] += dsigned
        dzr[pl.ds(0, RC, stride=16), :] = dsigned
        ddelta = dhalf * slope * 0.5
        dcosine = dhalf * delta * 0.5 * slope_d
        for j in range(NSUB):
            dzb[:, sub(j)] = gather_rows(dzr, 0, j, 16).astype(BF)

        zc[3] = nn(wcl[...], dzb[:, 0:PTS]).astype(BF) * dc[3]
        for l in range(3, 0, -1):
            zc[l - 1] = nn(w[5 + l], zc[l]).astype(BF) * dc[l - 1]
            acc[5 + l] += nt(hc[l - 1], zc[l])
            if last and l == 2:
                reduction.begin(0, grad_of(7), grad_of(8))
        dd = nn(wcx[...], zc[0]).astype(BF).astype(F32)
        for j in range(NSUB):
            spread_rows(dx, j, EROWS, dd[:, sub(j)])
        accx[...] += nt(fx[...], zc[0])
        accl[0] += nt(dzb[:, 0:PTS], hc[3, 0:H])
        fx[0:H] = nn(w[10], zc[0]).astype(BF)
        if last:
            reduction.begin(1, grad_of(6), turned(accx[0:H].astype(BF)))

        dpoint, dview = [], []
        for c in range(3):
            nb = ray_row(dx, 30 + c, EROWS) + dcosine * dcol[c]
            p = ray_row(dx, c, EROWS)
            v = ray_row(dx, 3 + c, EROWS) + dcosine * normal[c]
            eb[pl.ds(c, RC, stride=EROWS), :] = nb
            for k in range(6):
                two = 2.0**k
                sn, cs = feature(3 + 6 * k + c), feature(6 + 6 * k + c)
                eb[pl.ds(3 + 6 * k + c, RC, stride=EROWS), :] = two * cs * nb
                eb[pl.ds(6 + 6 * k + c, RC, stride=EROWS), :] = -two * sn * nb
                p = p - (two * two) * nb * (
                    sn * ray_row(de, 3 + 6 * k + c, EROWS) + cs * ray_row(de, 6 + 6 * k + c, EROWS)
                )
            for k in range(4):
                sn = xt[pl.ds(e0 + 6 + 6 * k + c, RC, stride=EROWS), :]
                cs = xt[pl.ds(e0 + 9 + 6 * k + c, RC, stride=EROWS), :]
                v = v + 2.0**k * (
                    cs * ray_row(dx, 6 + 6 * k + c, EROWS) - sn * ray_row(dx, 9 + 6 * k + c, EROWS)
                )
            dpoint.append(p)
            dview.append(v)

        for j in range(NSUB):
            encb[:, sub2(j)] = gather_rows(eb, 0, j, EROWS).astype(BF)
        for l in range(7):
            if l == 0:
                gg = nn(w0t[...], encb[:, PTS:])
            else:
                gg = nn(wt[l - 1], hx[l - 1, 0:H, PTS:])
            for j in range(NSUB):
                g = gg[:, sub(j)]
                s = ss[l, :, sub(j)]
                if l == 3:
                    g = g * s
                    x = g.astype(BF)
                else:
                    x = (g * s).astype(BF)
                s = s.astype(BF)
                u = wide(w7s[...]).astype(BF) if l == 6 else us[l, :, sub(j)]
                ts[l, :, sub(j)] = x * u * (2.0 - 2.0 * s)
                if l == 3:
                    e = gather_rows(eb, 0, j, EROWS)
                    x = ROOT_HALF * jnp.concatenate([g[0:EROWS] + e, g[EROWS:]], axis=0)
                    x = x.astype(BF)
                hx[l, 0:H, sub2(j)] = x
            if last and l == 6:
                reduction.step_a(0)

        dd = nn(w[9], fx[0:H])
        for j in range(NSUB):
            row = gather_rows(dzr, 0, j, 16)[0:1]
            d = dd[:, sub(j)] + wide(w7s[...]) * row
            zg[6, :, sub(j)] = d.astype(BF) * ss[6, :, sub(j)].astype(BF) + ts[6, :, sub(j)]
        acc[9] += nt(hx[6, :, 0:PTS], fx[0:H])
        accl[1] += nt(dzb[...], hx[6, 0:H])
        for l in range(6, 0, -1):
            dd = nn(w[l - 1], zg[l, :, 0:PTS])
            for j in range(NSUB):
                d = dd[:, sub(j)].astype(BF)
                if l == 4:
                    d = d.astype(F32) * ROOT_HALF
                    spread_rows(dx, j, EROWS, d)
                    d = d.astype(BF)
                zg[l - 1, :, sub(j)] = d * ss[l - 1, :, sub(j)].astype(BF) + ts[l - 1, :, sub(j)]
            acc[l - 1] += nt(hx[l - 1], zg[l])
            if last and l == 6:
                reduction.begin(2, acc[9, 0:H], grad_of(5))
                reduction.step_a(1)
            elif last and l == 4:
                reduction.begin(3, grad_of(4), grad_of(3))
            elif last and l == 3:
                reduction.step_a(2)
                reduction.step_b(0)
            elif last and l == 2:
                reduction.begin(4, acc[2, 0:H], grad_of(1))
        acc0[...] += nt(encb[...], zg[0])
        if last:
            finish_weights()
        dd = nn(w0[...], zg[0, :, 0:PTS]).astype(BF).astype(F32)
        for j in range(NSUB):
            spread_rows(dx, j, EROWS, dd[:, sub(j)] + gather_rows(dx, 0, j, EROWS))

        depth = dep[pl.ds(r0, RC), :]
        ddepth = jnp.zeros((RC, SAMP), F32)
        for c in range(3):
            p = dpoint[c] + ray_row(dx, c, EROWS)
            for k in range(6):
                p = p + 2.0**k * (
                    feature(6 + 6 * k + c) * ray_row(dx, 3 + 6 * k + c, EROWS)
                    - feature(3 + 6 * k + c) * ray_row(dx, 6 + 6 * k + c, EROWS)
                )
            ddepth = ddepth + p * dcol[c]
            v = dview[c] + depth * p
            out = out + jnp.where(lane128 == 3 + c, jnp.sum(p, axis=1, keepdims=True), 0.0)
            out = out + jnp.where(lane128 == 6 + c, jnp.sum(v, axis=1, keepdims=True), 0.0)
        outc[pl.ds(r0, RC), :] = out
        later = exact(ddepth, (iota((SAMP, SAMP), 0) >= iota((SAMP, SAMP), 1)).astype(F32))
        deltag_o[pl.ds(r0, RC), :] = ddelta + later - 0.5 * ddepth

    total = Total(place, tc, ta, tb, tz, town, tsend, trecv)

    def finish_weights():
        tail_rows = jnp.where(row8 == 0, accl[1, 0:8], accl[0, 0:8])
        lines = [acc[0, H : H + 1]]
        for k in (0, 1, 4, 5, 3, 0, 6, 7, 8):
            lines.append(acc[k, H : H + 1])
        small_rows = jnp.concatenate(lines, axis=0)
        upper = jnp.concatenate(
            [
                acc0[...],
                jnp.zeros((CROSS - EROWS, H), F32),
                accx[H : H + EROWS],
                jnp.zeros((BIASES - CROSS - EROWS, H), F32),
                small_rows,
                jnp.zeros((TAIL - BIASES - 10, H), F32),
                tail_rows,
                jnp.zeros((H - TAIL - 8, H), F32),
            ],
            axis=0,
        )
        packed = turned(upper.astype(BF))
        reduction.begin(5, grad_of(0), packed)

        def amount(k):
            return jnp.sum(jnp.sum(vac[k], axis=1, keepdims=True), axis=0, keepdims=True)

        lane_bias = jnp.zeros((1, H), F32)
        for k in range(4):
            lane_bias = lane_bias + jnp.where(lane256 == TAIL + k, amount(1 + k), 0.0)
        variance = jnp.where(lane256 == 0, amount(0) * inv_s * 10.0, 0.0)
        sums = jnp.concatenate(
            [
                jnp.sum(d3 * acc[2, 0:H], axis=0, keepdims=True),
                acc[2, H : H + 1],
                jnp.sum(d7 * acc[9, 0:H], axis=0, keepdims=True),
                acc[9, H : H + 1],
                jnp.sum(misc * packed, axis=0, keepdims=True),
                lane_bias,
                variance,
                jnp.zeros((1, H), F32),
            acc0[ENC : ENC + 1],
            *lines[1:6],
            accx[H + NX : H + NX + 1],
            *lines[7:],
            jnp.zeros((TOT - 18, H), F32),
            ],
            axis=0,
        )
        total.begin(sums)

    each(0, rays // RC - 1, lambda i: chunk(i, False))
    chunk(rays // RC - 1, True)

    reduction.step_a(3)
    reduction.step_b(1)
    reduction.step_a(4)
    total.go_on(0)
    reduction.step_a(5)
    reduction.step_b(2)
    reduction.step_z(0)
    reduction.step_b(3)
    total.go_on(1)
    reduction.step_z(1)
    reduction.step_b(4)
    reduction.step_z(2)
    reduction.step_b(5)
    total.go_on(2)
    result = outc[...].T
    rgb_o[...] = result[0:3, 0:rays]
    ag_o[...] = result[3:6, 0:rays]
    dg_o[...] = result[6:9, 0:rays]
    for q in range(3, 6):
        reduction.step_z(q)
    for q in range(5):
        reduction.step_end(q)
    tot_o[...] = total.end()
    reduction.step_end(5)
    for q in range(6):
        reduction.settle(q)


def compute(fsdp, devices, anchors, directions, deltas, foreground, cotangent, smalls, layers):
    rays = deltas.shape[0]
    vm, dma = pltpu.VMEM, pltpu.SemaphoreType.DMA
    rp = layers[0].shape[0]
    points = rays * EROWS
    RC = 8 if devices <= 32 else 4
    PTS = RC * SAMP
    depth = fsdp // 2
    scratch = [
        vm((6, devices, 2 * rp, H), BF),
        vm((4, rp, 384), F32),
        dma((2, devices)),
        dma((2, devices)),
        vm((6, 2, 2 * depth, 2 * rp, H), BF),
        vm((6, 2 * depth, 2 * rp, H), BF),
        vm((6, depth, 2 * rp, H), BF),
        vm((6, depth, 2 * rp, H), BF),
        dma((6, 3 + depth)),
        dma((6, 2)),
        dma((6,)),
        dma((6,)),
        dma((6, depth)),
        vm((TOT, H), F32),
        vm((TOT, H), F32),
        vm((TOT, H), F32),
        vm((depth, TOT, H), F32),
        vm((3, TOT, H), F32),
        dma((2 + depth,)),
        dma((2 + depth,)),
        vm((GROUPS, H, H), BF),
        vm((8, 384), F32),
        vm((9, H, H), BF),
        vm((11, H, H), BF),
        vm((H + 16, H), BF),
        vm((H, EROWS), BF),
        vm((EROWS, H), BF),
        vm((H, H + EROWS), BF),
        vm((EROWS, H), BF),
        vm((16, H), BF),
        vm((H, 16), BF),
        vm((H, 128), F32),
        vm((10, H, 128), F32),
        vm((points, SAMP), F32),
        vm((ENC, rays, SAMP), F32),
        vm((points, SAMP), F32),
        vm((rays, SAMP), F32),
        vm((128, 128), F32),
        vm((7, H + 16, 2 * PTS), BF),
        vm((7, H, PTS), F32),
        vm((6, H, PTS), BF),
        vm((7, H, 2 * PTS), BF),
        vm((7, H, PTS), BF),
        vm((H + EROWS, PTS), BF),
        vm((4, H + 16, PTS), BF),
        vm((4, H, PTS), BF),
        vm((4, H, PTS), BF),
        vm((EROWS, 2 * PTS), BF),
        vm((16, 2 * PTS), BF),
        vm((RC * EROWS, SAMP), F32),
        vm((RC * EROWS, SAMP), F32),
        vm((RC * 16, SAMP), F32),
        vm((RC * 16, SAMP), F32),
        vm((RC * 16, SAMP), F32),
        vm((RC * EROWS, SAMP), F32),
        vm((RC * EROWS, SAMP), F32),
        vm((128, 128), F32),
        vm((10, H + 16, H), F32),
        vm((EROWS, H), F32),
        vm((H + EROWS, H), F32),
        vm((2, 16, H), F32),
        vm((5, RC, SAMP), F32),
    ]
    shapes = (
        jax.ShapeDtypeStruct((3, rays), F32),
        jax.ShapeDtypeStruct((3, rays), F32),
        jax.ShapeDtypeStruct((3, rays), F32),
        jax.ShapeDtypeStruct((rays, SAMP), F32),
        jax.ShapeDtypeStruct((GROUPS * rp, H), F32),
        jax.ShapeDtypeStruct((TOT, H), F32),
        jax.ShapeDtypeStruct((8, H), F32),
        jax.ShapeDtypeStruct((8, H), F32),
    )
    whole = pl.BlockSpec(memory_space=pltpu.VMEM)
    return pl.pallas_call(
        functools.partial(compute_kernel, fsdp, RC),
        out_shape=shapes,
        in_specs=[whole] * 30,
        out_specs=(whole,) * 8,
        scratch_shapes=scratch,
        name="nets",
        compiler_params=pltpu.CompilerParams(
            collective_id=0, has_side_effects=True, vmem_limit_bytes=62 * 1024 * 1024
        ),
    )(anchors, directions, deltas, foreground, cotangent, *smalls, *layers)


def unscaled_rows(d, gain, grad):
    inv = lax.rsqrt(jnp.sum(d * d, axis=1, keepdims=True) + EPS)
    dot = jnp.sum(d * grad, axis=1, keepdims=True)
    return grad * (gain * inv) - d * (gain * inv * inv * inv * dot), dot * inv


def finish_kernel(
    real, share, tot, inv, smalls, first, mid, narrow, skip, last, cfirst, cmid,
    fg, mg, sg, cg, cmg, cl, rgb, ag, dg, deltag, o_rgb, o_ag, o_dg, o_deltag,
    o_first, o_fg, o_fb, o_mid, o_mg, o_mb, o_narrow, o_ng, o_nb, o_skip, o_sg, o_sb,
    o_last, o_lg, o_lb, o_cfirst, o_cg, o_cb, o_cmid, o_cmg, o_cmb, o_clast, o_clg, o_clb, o_var,
    wid,
):
    r = first.shape[0]
    for src, dst in ((rgb, o_rgb), (ag, o_ag), (dg, o_dg), (deltag, o_deltag)):
        dst[...] = src[...]
    d_first, d_narrow, d_last, d_cfirst = share_rows(first, narrow, last, cfirst, wid)

    def vec(ref, k=None):
        return column(as_row(ref) if k is None else ref[...].astype(F32)[k : k + 1])

    def group(k):
        at = [g for pair in PAIRS for g in pair].index(k)
        return share[at * r : (at + 1) * r, :]

    def put(ref, col):
        ref[...] = line(col).reshape(r)

    def put_rows(ref, columns):
        ref[...] = jnp.concatenate([line(col) for col in columns], axis=0)

    first_unit = (lax.axis_index("fsdp") * 4 + lax.axis_index("rep")) * real
    mine = iota((r, H), 1) == first_unit + iota((r, H), 0)

    def bias(j):
        return jnp.sum(jnp.where(mine, tot[8 + j : 9 + j, :], 0.0), axis=1, keepdims=True)

    misc = group(9)
    lane = iota((1, 128), 1)
    g, gain = unscaled_rows(d_first, vec(fg), jnp.where(lane < ENC, misc[:, 0:128], 0.0))
    o_first[...] = g[:, 0:ENC]
    put(o_fg, gain)
    put(o_fb, bias(0))
    gains = []
    for k in range(4):
        g, gain = unscaled_rows(mid[k].astype(F32), vec(mg, k), group(k))
        o_mid[k] = g
        gains.append(gain)
    put_rows(o_mg, gains)
    put_rows(o_mb, [bias(1 + k) for k in range(4)])
    g, gain = unscaled_rows(skip[...].astype(F32), vec(sg), pltpu.roll(group(4), H - ENC, 1))
    o_skip[...] = g
    put(o_sg, gain)
    put(o_sb, bias(5))
    extra = jnp.where(lane < NX, misc[:, 128:256], 0.0)
    moved = jnp.concatenate([group(8), jnp.zeros((r, 128), F32)], axis=1)
    grad = pltpu.roll(moved, NX, 1) + jnp.concatenate([extra, jnp.zeros((r, H), F32)], axis=1)
    g, gain = unscaled_rows(d_cfirst, vec(cg), grad)
    o_cfirst[...] = g[:, 0 : H + NX]
    put(o_cg, gain)
    put(o_cb, bias(6))
    gains = []
    for k in range(3):
        g, gain = unscaled_rows(cmid[k].astype(F32), vec(cmg, k), group(5 + k))
        o_cmid[k] = g
        gains.append(gain)
    put_rows(o_cmg, gains)
    put_rows(o_cmb, [bias(7 + k) for k in range(3)])

    def across(k, d, grad):
        gain, iv, dot = smalls[k : k + 1, :], inv[k : k + 1, :], tot[k : k + 1, :]
        return grad * (gain * iv) - d * (gain * iv * iv * iv * dot)

    g = across(0, pltpu.roll(d_narrow, ENC, 1), group(10))
    o_narrow[...] = pltpu.roll(g, H - ENC, 1)[:, 0:NARROW]
    g = across(2, pltpu.roll(d_last, 383, 1)[:, 0:H], group(11))
    right = jnp.where(lane == TAIL - 128, d_last[:, 0:1], 0.0)
    for c in range(3):
        right = right + jnp.where(lane == TAIL - 127 + c, vec(cl, c), 0.0)
    t = across(4, jnp.concatenate([jnp.zeros((r, 128), F32), right], axis=1), misc)
    first_lane = iota((1, 384), 1) == 0

    def behind(x, front):
        more = jnp.zeros((x.shape[0], 128), F32)
        moved = pltpu.roll(jnp.concatenate([x, more], axis=1), 1, 1)
        return jnp.where(first_lane, front, moved)[:, 0 : H + 1]

    o_last[...] = behind(g, t[:, TAIL : TAIL + 1])
    put_rows(o_clast, [t[:, TAIL + 1 + c : TAIL + 2 + c] for c in range(3)])
    gained = tot[0:8, :] * inv[...]
    back = pltpu.roll(jnp.concatenate([gained[0:1], tot[1:2], jnp.zeros((6, H), F32)], axis=0), H - ENC, 1)
    o_ng[...] = back[0:1, 0:NARROW].reshape(NARROW)
    o_nb[...] = back[1:2, 0:NARROW].reshape(NARROW)
    eight = jnp.zeros((7, H), F32)
    o_lg[...] = behind(jnp.concatenate([gained[2:3], eight], axis=0), gained[4:5, TAIL : TAIL + 1])[0:1].reshape(H + 1)
    o_lb[...] = behind(jnp.concatenate([tot[3:4], eight], axis=0), tot[5:6, TAIL : TAIL + 1])[0:1].reshape(H + 1)
    tails = jnp.concatenate([gained[4:5], tot[5:6], jnp.zeros((6, H), F32)], axis=0)
    tails = pltpu.roll(tails, H - TAIL - 1, 1)
    o_clg[...] = tails[0:1, 0:3].reshape(3)
    o_clb[...] = tails[1:2, 0:3].reshape(3)
    o_var[...] = tot[6:7, 0:1].reshape(1)


def per_device(
    fsdp, devices,
    anchors, directions, deltas, foreground,
    sdf_first_dir, sdf_first_gain, sdf_first_bias,
    sdf_mid_dir, sdf_mid_gain, sdf_mid_bias,
    sdf_narrow_dir, sdf_narrow_gain, sdf_narrow_bias,
    sdf_skip_dir, sdf_skip_gain, sdf_skip_bias,
    sdf_last_dir, sdf_last_gain, sdf_last_bias,
    color_first_dir, color_first_gain, color_first_bias,
    color_mid_dir, color_mid_gain, color_mid_bias,
    color_last_dir, color_last_gain, color_last_bias,
    variance, rgb_cotangent,
):
    r = sdf_first_gain.shape[0]
    rp = max(r, 8)
    whole = pl.BlockSpec(memory_space=pltpu.VMEM)

    def rows(x):
        return x if rp == r else jnp.pad(x, [(0, 0)] * (x.ndim - 2) + [(0, rp - r), (0, 0)])

    def lanes(x):
        return x if rp == r else jnp.pad(x, [(0, 0)] * (x.ndim - 1) + [(0, rp - r)])

    shares = (
        rows(sdf_first_dir.T),
        rows(jnp.swapaxes(sdf_mid_dir, 1, 2)),
        rows(sdf_narrow_dir),
        rows(sdf_skip_dir.T),
        rows(sdf_last_dir),
        rows(color_first_dir.T),
        rows(jnp.swapaxes(color_mid_dir, 1, 2)),
    )
    fg, fb, mg, mb, sg, sb, cg, cb, cmg, cmb, cl = (
        lanes(x)
        for x in (
            sdf_first_gain, sdf_first_bias, sdf_mid_gain, sdf_mid_bias, sdf_skip_gain, sdf_skip_bias,
            color_first_gain, color_first_bias, color_mid_gain, color_mid_bias, color_last_dir.T,
        )
    )
    rgb, ag, dg, deltag, share, tot, inv, smalls = compute(
        fsdp, devices, anchors, directions, deltas, foreground, rgb_cotangent,
        (
            variance, sdf_narrow_gain, sdf_narrow_bias, sdf_last_gain, sdf_last_bias,
            color_last_gain, color_last_bias,
        ),
        (*shares, fg, fb, mg, mb, sg, sb, cg, cb, cmg, cmb, cl),
    )
    def f32(*shape):
        return jax.ShapeDtypeStruct(shape, F32)

    outs = pl.pallas_call(
        functools.partial(finish_kernel, r),
        out_shape=(
            f32(*rgb.shape), f32(*ag.shape), f32(*dg.shape), f32(*deltag.shape),
            f32(rp, ENC), f32(rp), f32(rp),
            f32(4, rp, H), f32(4, rp), f32(4, rp),
            f32(rp, NARROW), f32(NARROW), f32(NARROW),
            f32(rp, H), f32(rp), f32(rp),
            f32(rp, H + 1), f32(H + 1), f32(H + 1),
            f32(rp, H + NX), f32(rp), f32(rp),
            f32(3, rp, H), f32(3, rp), f32(3, rp),
            f32(3, rp), f32(3), f32(3),
            f32(1),
        ),
        in_specs=[whole] * 21,
        out_specs=(whole,) * 29,
        scratch_shapes=[pltpu.VMEM((4, rp, 384), F32)],
        name="finish",
    )(share, tot, inv, smalls, *shares, fg, mg, sg, cg, cmg, cl, rgb, ag, dg, deltag)
    (
        rgb, ag, dg, deltag,
        o_first, o_fg, o_fb, o_mid, o_mg, o_mb, o_narrow, o_ng, o_nb, o_skip, o_sg, o_sb,
        o_last, o_lg, o_lb, o_cfirst, o_cg, o_cb, o_cmid, o_cmg, o_cmb, o_clast, o_clg, o_clb, o_var,
    ) = outs
    return (
        rgb, ag, dg, deltag,
        o_first[0:r].T, o_fg[0:r], o_fb[0:r],
        jnp.swapaxes(o_mid[:, 0:r], 1, 2), o_mg[:, 0:r], o_mb[:, 0:r],
        o_narrow[0:r], o_ng, o_nb,
        o_skip[0:r].T, o_sg[0:r], o_sb[0:r],
        o_last[0:r], o_lg, o_lb,
        o_cfirst[0:r].T, o_cg[0:r], o_cb[0:r],
        jnp.swapaxes(o_cmid[:, 0:r], 1, 2), o_cmg[:, 0:r], o_cmb[:, 0:r],
        o_clast[:, 0:r].T, o_clg, o_clb,
        o_var,
    )


def solution(mesh):
    fsdp, rep = mesh.shape["fsdp"], mesh.shape["rep"]
    assert rep == 4 and fsdp % 2 == 0
    both = ("fsdp", "rep")
    cols, vec, cols3, rows, copied = P(None, both), P(both), P(None, None, both), P(both, None), P()
    layers = (
        cols, vec, vec, cols3, cols, cols, rows, copied, copied, cols, vec, vec,
        rows, copied, copied, cols, vec, vec, cols3, cols, cols, rows, copied, copied,
    )
    return jax.shard_map(
        functools.partial(per_device, fsdp, fsdp * rep),
        mesh=mesh,
        in_specs=(cols, cols, rows, rows) + layers + (copied, cols),
        out_specs=(cols, cols, cols, rows) + layers + (copied,),
        check_vma=False,
    )
```
